128 devices in a mesh: lat: 8 (over x_hi, y), lon: 16 (over x_lo, z, core).
Axes of the slice: x: 4 (x_hi: 2, x_lo: 2; x = x_hi * 2 + x_lo), y: 4, z: 4, core: 2. Of those that a mesh axis runs over, the one named last changes fastest.
Arguments:
- tokens: bfloat16 [32768, 1024], P(('lat', 'lon')), may hold values from -8 to 8
- attn_gain: float32 [1024], replicated, may hold values from 0.1 to 1.9
- w_query: bfloat16 [1024, 1024], replicated, may hold values from -1 to 1
- w_key: bfloat16 [1024, 256], replicated, may hold values from -4 to 4
- w_value: bfloat16 [1024, 256], replicated, may hold values from -0.1875 to 0.1875
- w_out: bfloat16 [1024, 1024], replicated, may hold values from -0.1875 to 0.1875
- head_rate: float32 [16], replicated, may hold values from 0.00024414062 to 0.05
- obs_values: bfloat16 [16384, 128, 32], P(('lat', 'lon')), may hold values from -6 to 6
- tile_owner: int32 [16384, 1], P(('lat', 'lon')), may hold values from 0 to 127; in each aligned block of 128 rows (0 to 127, 128 to 255, ...) at most 2 rows name the same one
- tile_cell: int32 [16384], P(('lat', 'lon')), may hold values from 0 to 255
- tile_count: int32 [16384], P(('lat', 'lon')), may hold values from 1 to 128
- w_obs_in: bfloat16 [32, 1024], replicated, may hold values from -1 to 1
- w_obs_out: bfloat16 [1024, 1024], replicated, may hold values from -0.1875 to 0.1875
- mlp_gain: float32 [1024], replicated, may hold values from 0.1 to 1.9
- w_up: bfloat16 [1024, 4096], replicated, may hold values from -0.1875 to 0.1875
- w_down: bfloat16 [4096, 1024], replicated, may hold values from -0.09375 to 0.09375
Outputs:
- updated: bfloat16 [32768, 1024], P(('lat', 'lon'))
The draws below stay inside these ranges and needn't reach their ends.
Inputs may be any that keep to these rules, and one draw needn't show every extreme that they name: `tile_owner`: the 128 tiles of one device name one owner at most 2 times; some owner is named exactly 2 times by some device.
All inputs are finite; a program needn't handle non-finite values.
Results may differ from the reference program's by a relative error of at most 0.0095.
The reference program's roundings to bfloat16 on the way count: a program that leaves them out, or rounds other values in their place, can miss the bound.
Values may be sent and summed in bfloat16 or wider, within the bound.
No kernel may reach another device: no remote copies, remote signals or barrier semaphores. Data moves between devices by JAX's collectives and lax.ppermute only.
A program may use at most 128 MiB of HBM per device.

```python
import math
import jax
import jax.numpy as jnp
import numpy as np
from jax import lax

D = 1024
HEADS = 16
HD = 64
KVH = 4
FF = 4096
F_OBS = 32
TROWS = 128
TOK_DEV = 256
TILE_DEV = 128
CAP = 2
TOKENS = 32768
TILES = 16384
N_LAT = 8
N_LON = 16


def draw_tokens(key, part):
    base_draw = jax.random.normal(key, (TOKENS, D), jnp.float32)
    return jnp.clip(base_draw, -8.0, 8.0).astype(jnp.bfloat16)


def query_key_pair(key):
    key_one, key_two = jax.random.split(jax.random.fold_in(key, 7), 2)
    spread = 1.6 / math.sqrt(D)
    query_draw = jax.random.normal(key_one, (D, HEADS * HD), jnp.float32) * spread
    key_draw = jax.random.normal(key_two, (D, KVH * HD), jnp.float32) * spread
    return (jnp.clip(query_draw, -1.0, 1.0), jnp.clip(key_draw, -4.0, 4.0))


def draw_w_query(key, part):
    return query_key_pair(key)[0].astype(jnp.bfloat16)


def draw_w_key(key, part):
    return query_key_pair(key)[1].astype(jnp.bfloat16)


def place_ends(result, key, low, largest):
    shape = result.shape
    index_at = [jax.random.randint(jax.random.fold_in(key, axis), (), 0, shape[axis]) for axis in range(len(shape))]
    result = result.at[tuple(index_at)].set(low)
    longest = shape.index(max(shape))
    index_at[longest] = (index_at[longest] + 1) % shape[longest]
    return result.at[tuple(index_at)].set(largest)


def levels(rng, dims, cuts, low, top_value):
    gain = 1.0
    for position, blocks in cuts:
        heights = jax.random.uniform(jax.random.fold_in(jax.random.fold_in(rng, 6), position), (blocks,), jnp.float32, low / len(cuts), top_value / len(cuts))
        gain = gain * jnp.repeat(jnp.exp(heights), dims[position] // blocks).reshape((-1,) + (1,) * (len(dims) - 1 - position))
    return gain


def shared_out(own_key, own, number, rows, number_of, top, most, lean):
    ranking = jax.random.permutation(own_key, number_of)
    crowded, ordinary = load_shares(number_of, rows * top, most, lean, True), load_shares(number_of, rows * top, most, lean, False)
    places = jnp.arange(number_of)

    def named(lengths, offset_by):
        used = int((lengths > 0).sum())
        fixed = max(1, used // 4)
        shifted = fixed + (places - fixed + offset_by * (used - fixed)) % max(1, number_of - fixed)
        return jnp.zeros((number_of,), jnp.int32).at[ranking[jnp.where(places < fixed, places, shifted)]].set(jnp.asarray(lengths, jnp.int32))

    lengths = jnp.where(number % 4 == 0, named(crowded, number // 4), named(ordinary, number - number // 4 - 1))
    mixed = jax.random.permutation(jax.random.fold_in(own, 3), number_of)
    source_of, taker = mixed[0:number_of // 2 * 2:2], mixed[1:number_of // 2 * 2:2]
    room = jnp.minimum(lengths[source_of] - 1, most - lengths[taker]) // 2
    room = jnp.where((source_of == ranking[0]) | (taker == ranking[0]) | (lengths[taker] == 0), 0, jnp.maximum(room, 0))
    shifted = jax.random.randint(jax.random.fold_in(own, 4), (number_of // 2,), 0, 1 << 20) % (room + 1)
    lengths = lengths.at[source_of].add(-shifted).at[taker].add(shifted)
    labels = jnp.searchsorted(jnp.cumsum(lengths), jnp.arange(rows * top), side="right").astype(jnp.int32)
    listing = labels.reshape(top, rows).T
    listing = listing[jax.random.permutation(jax.random.fold_in(own, 1), rows)]
    offset_by = jax.random.randint(jax.random.fold_in(own, 2), (rows, 1), 0, top)
    return jnp.take_along_axis(listing, (jnp.arange(top)[None, :] + offset_by) % top, axis=1)


def load_shares(number_of, total, limit, slope, full):
    weights = [(1 << 20) // math.isqrt(grade ** slope) + 1 for grade in range(1, number_of + 1)]
    largest = limit if full else min(limit, max(-(-total // number_of), total * weights[0] // sum(weights)))
    least = 1 if total - largest >= number_of - 1 else 0
    counts, rest = [largest] + [least] * (number_of - 1), total - largest - least * (number_of - 1)
    while rest > 0:
        movable = [i for i in range(1, number_of) if counts[i] < largest] or [i for i in range(1, number_of) if counts[i] < limit]
        mass, budget = sum([weights[i] for i in movable]), rest
        for i in movable:
            addition = min(limit - counts[i], max(1, budget * weights[i] // mass), rest)
            counts[i] = counts[i] + addition
            rest = rest - addition
    return np.array(counts)


def gaussian(rng, shape, scale, reach, pieces=(), kind=jnp.bfloat16):
    result = jax.random.normal(rng, shape, jnp.float32) * scale
    if len(pieces) > 0:
        result = levels(rng, shape, pieces, -0.22, 0.18) * result
    return jnp.clip(result, min=-reach, max=reach).astype(kind)


def setup_inputs(seed: int = 0) -> dict:
    streams_of = jax.random.split(jax.random.key(seed), 17)
    tokens = draw_tokens(jax.random.fold_in(streams_of[16], 71), 0)
    attn_gain = jnp.clip(1.0 + 0.18 * jax.random.normal(streams_of[1], (D,), jnp.float32), 0.1, 1.9)
    w_query = draw_w_query(jax.random.fold_in(streams_of[16], 71), 0)
    w_key = draw_w_key(jax.random.fold_in(streams_of[16], 71), 0)
    w_value = gaussian(streams_of[4], (D, KVH * HD), D ** -0.5, 0.1875)
    w_out = gaussian(streams_of[5], (HEADS * HD, D), (HEADS * HD) ** -0.5, 0.1875)
    head_rate = jnp.clip(jnp.exp(jax.random.uniform(streams_of[6], (HEADS,), jnp.float32, math.log(0.00024414062), math.log(0.05))), 0.00024414062, 0.05)
    obs_values = gaussian(streams_of[7], (TILES, TROWS, F_OBS), 1.0, 6.0, ((0, 128),))
    tile_owner_keys = jax.random.split(jax.random.fold_in(streams_of[8], 1), TILES // TILE_DEV)
    tile_owner_turns = jax.random.permutation(jax.random.fold_in(streams_of[8], 3), TILES // TILE_DEV)
    tile_owner = jax.vmap(lambda own, number: shared_out(jax.random.fold_in(streams_of[8], 2), own, number, TILE_DEV, N_LAT * N_LON, 1, CAP, 2))(tile_owner_keys, tile_owner_turns).reshape((TILES, 1))
    tile_cell = place_ends(jax.random.randint(streams_of[9], (TILES,), 0, TOK_DEV), jax.random.fold_in(streams_of[9], 1), 0, TOK_DEV - 1).astype(jnp.int32)
    tile_count = place_ends(jax.random.randint(streams_of[10], (TILES,), 1, TROWS + 1), jax.random.fold_in(streams_of[10], 1), 1, TROWS).astype(jnp.int32)
    w_obs_in = gaussian(streams_of[11], (F_OBS, D), F_OBS ** -0.5, 1.0)
    w_obs_out = gaussian(streams_of[12], (D, D), D ** -0.5, 0.1875)
    mlp_gain = jnp.clip(1.0 + 0.18 * jax.random.normal(streams_of[13], (D,), jnp.float32), 0.1, 1.9)
    w_up = gaussian(streams_of[14], (D, FF), D ** -0.5, 0.1875)
    w_down = gaussian(streams_of[15], (FF, D), FF ** -0.5, 0.09375)
    return dict(tokens=tokens, attn_gain=attn_gain, w_query=w_query, w_key=w_key, w_value=w_value, w_out=w_out, head_rate=head_rate, obs_values=obs_values, tile_owner=tile_owner, tile_cell=tile_cell, tile_count=tile_count, w_obs_in=w_obs_in, w_obs_out=w_obs_out, mlp_gain=mlp_gain, w_up=w_up, w_down=w_down)


def scaled_rows(row_data, row_gain):
    as_float = row_data.astype(jnp.float32)
    mean_square = lax.optimization_barrier(jnp.mean(as_float * as_float, axis=-1, keepdims=True))
    return (as_float * lax.rsqrt(mean_square + 1e-05) * row_gain).astype(jnp.bfloat16)

def pool_tiles(obs_tiles, tile_counts, w_obs_in):
    tile_total, tile_rows, feature_count = obs_tiles.shape
    block_rows = math.gcd(tile_total, 32)

    def one_block(block_args):
        value_block, count_block = block_args
        activity = jax.nn.gelu(jnp.dot(value_block.reshape(block_rows * tile_rows, feature_count), w_obs_in, preferred_element_type=jnp.float32))
        activity = activity.reshape(block_rows, tile_rows, -1)
        live_rows = (jnp.arange(tile_rows, dtype=jnp.int32)[None, :] < count_block[:, None]).astype(jnp.float32)
        summed = lax.optimization_barrier(jnp.sum(activity * live_rows[:, :, None], axis=1))
        return (summed / jnp.maximum(count_block, 1).astype(jnp.float32)[:, None]).astype(jnp.bfloat16)
    pooled = lax.map(one_block, (obs_tiles.reshape(tile_total // block_rows, block_rows, tile_rows, feature_count), tile_counts.reshape(tile_total // block_rows, block_rows)))
    return pooled.reshape(tile_total, -1)

def band_attention(query_rows, key_rows, value_rows, head_rate):
    band_rows = TOK_DEV * N_LON
    group_size = HEADS // KVH
    block_rows = math.gcd(band_rows, 512)
    inv_scale = 1.0 / math.sqrt(HD)
    key_float = key_rows.astype(jnp.float32).reshape(band_rows, KVH, HD)
    value_float = value_rows.astype(jnp.float32).reshape(band_rows, KVH, HD)
    rate_table = head_rate.reshape(KVH, group_size)
    key_position = jnp.arange(band_rows, dtype=jnp.int32)

    def one_block(block_first):
        query_block = lax.dynamic_slice_in_dim(query_rows, block_first, block_rows, 0).astype(jnp.float32).reshape(block_rows, KVH, group_size, HD)
        scores = jnp.einsum('qkgd,skd->kgqs', query_block, key_float) * inv_scale
        distance = jnp.abs((block_first + jnp.arange(block_rows, dtype=jnp.int32))[:, None] - key_position[None, :])
        distance = jnp.minimum(distance, band_rows - distance).astype(jnp.float32)
        scores = scores - rate_table[:, :, None, None] * distance[None, None]
        row_top = lax.optimization_barrier(jnp.max(scores, axis=-1, keepdims=True))
        weights = jnp.exp(scores - row_top)
        weight_sum = lax.optimization_barrier(jnp.sum(weights, axis=-1))
        rounded_weights = lax.optimization_barrier(weights.astype(jnp.bfloat16)).astype(jnp.float32)
        context = jnp.einsum('kgqs,skd->qkgd', rounded_weights, value_float) / jnp.transpose(weight_sum, (2, 0, 1))[..., None]
        return context.reshape(block_rows, HEADS * HD).astype(jnp.bfloat16)
    block_starts = jnp.arange(band_rows // block_rows, dtype=jnp.int32) * block_rows
    return lax.map(one_block, block_starts).reshape(band_rows, HEADS * HD)

def reference(tokens, attn_gain, w_query, w_key, w_value, w_out, head_rate, obs_values, tile_owner, tile_cell, tile_count, w_obs_in, w_obs_out, mlp_gain, w_up, w_down):
    normed = scaled_rows(tokens, attn_gain)
    query_rows = jnp.dot(normed, w_query, preferred_element_type=jnp.float32).astype(jnp.bfloat16)
    key_rows = jnp.dot(normed, w_key, preferred_element_type=jnp.float32).astype(jnp.bfloat16)
    value_rows = jnp.dot(normed, w_value, preferred_element_type=jnp.float32).astype(jnp.bfloat16)
    band_rows = TOK_DEV * N_LON

    def one_band(band_args):
        return band_attention(band_args[0], band_args[1], band_args[2], head_rate)
    context = lax.map(one_band, (query_rows.reshape(N_LAT, band_rows, -1), key_rows.reshape(N_LAT, band_rows, -1), value_rows.reshape(N_LAT, band_rows, -1)))
    context = context.reshape(TOKENS, HEADS * HD)
    attended = jnp.dot(context, w_out, preferred_element_type=jnp.float32)
    pooled = pool_tiles(obs_values, tile_count, w_obs_in)
    increment = jnp.dot(pooled, w_obs_out, preferred_element_type=jnp.float32)
    target = (tile_owner[:, 0] * TOK_DEV + tile_cell).astype(jnp.int32)
    update = jax.ops.segment_sum(increment, target, num_segments=TOKENS)
    mixed_rows = (tokens.astype(jnp.float32) + attended + update).astype(jnp.bfloat16)
    mixed_rows = lax.optimization_barrier(mixed_rows)
    normed_mlp = scaled_rows(mixed_rows, mlp_gain)
    hidden = jax.nn.gelu(jnp.dot(normed_mlp, w_up, preferred_element_type=jnp.float32)).astype(jnp.bfloat16)
    return (mixed_rows.astype(jnp.float32) + jnp.dot(hidden, w_down, preferred_element_type=jnp.float32)).astype(jnp.bfloat16)
```

```python
import functools
import math

import jax
import jax.numpy as jnp
from jax import lax
from jax.experimental import pallas as pl
from jax.experimental.pallas import tpu as pltpu
from jax.sharding import PartitionSpec as P

BF = jnp.bfloat16
F32 = jnp.float32
I32 = jnp.int32

D = 1024
HEADS = 16
HD = 64
KVH = 4
FF = 4096
ROWS = 256
TILES = 128
TROWS = 128
F_OBS = 32
LON = 16
BAND = ROWS * LON
SLOTS = 256
PAY = D + 128
LOG2E = 1.4426950408889634
VT = HD + 16
MIB = 2**20
VMEM = pl.BlockSpec(memory_space=pltpu.VMEM)
SMEM = pl.BlockSpec(memory_space=pltpu.SMEM)
ANY = pl.BlockSpec(memory_space=pl.ANY)


def iota(shape, dim):
    return lax.broadcasted_iota(I32, shape, dim)


def params(mib):
    return pltpu.CompilerParams(vmem_limit_bytes=mib * MIB)


def cost(micros):
    return pl.CostEstimate(
        flops=int(micros * 1.0e9), bytes_accessed=int(micros * 1.0e6), transcendentals=0
    )


def dot(a, b):
    return jnp.dot(a, b, preferred_element_type=F32)


def normed_rows(rows, gain):
    mean_square = jnp.mean(rows * rows, axis=-1, keepdims=True)
    return (rows * lax.rsqrt(mean_square + 1e-05) * gain).astype(BF)


def twice_gelu(x):
    k0 = math.sqrt(2.0 / math.pi)
    k1 = k0 * 0.044715
    inner = x * (x * x * k1 + k0)
    return jnp.tanh(inner) * x + x


def kv_kernel(tok_ref, gain_ref, wk_ref, wv_ref, normed_ref, kv_ref):
    normed = normed_rows(tok_ref[...].astype(F32), gain_ref[...])
    normed_ref[...] = normed
    kv_ref[0:ROWS, :] = dot(normed, wk_ref[...]).astype(BF)
    kv_ref[ROWS : 2 * ROWS, :] = dot(normed, wv_ref[...]).T.astype(BF)


def kv_call(tokens, gain, w_key, w_value):
    return pl.pallas_call(
        kv_kernel,
        out_shape=(
            jax.ShapeDtypeStruct((ROWS, D), BF),
            jax.ShapeDtypeStruct((2 * ROWS, KVH * HD), BF),
        ),
        in_specs=[VMEM] * 4,
        out_specs=(VMEM, VMEM),
        compiler_params=params(16),
        cost_estimate=cost(3),
        name="norm_keys_values",
    )(tokens, gain.reshape(1, D), w_key, w_value)


def pool_kernel(cnt_s, obs_ref, cnt_ref, own_ref, cell_ref, w_ref, pay_ref, live_ref, acc_ref):
    def put(tile, first):
        live_ref[pl.ds(pl.multiple_of(first, 16), TROWS), :] = obs_ref[tile]
        return first + ((cnt_s[tile] + 15) // 16) * 16

    total = lax.fori_loop(0, TILES, put, jnp.int32(0))
    live_ref[pl.ds(pl.multiple_of(total, 16), ROWS), :] = jnp.zeros((ROWS, F_OBS), BF)

    square = (TILES, TILES)
    cnt = jnp.broadcast_to(cnt_ref[...].astype(F32), square).T
    groups = jnp.floor((cnt + 15.0) * (1.0 / 16.0))
    earlier = (iota(square, 1) < iota(square, 0)).astype(F32)
    start = dot(earlier.astype(BF), groups.astype(BF)) * 16.0
    start = jnp.concatenate([start, start], axis=1).astype(I32)
    live = jnp.concatenate([cnt, cnt], axis=1).astype(I32)

    acc_ref[...] = jnp.zeros_like(acc_ref)

    @pl.loop(0, (total + ROWS - 1) // ROWS)
    def _(block):
        first = pl.multiple_of(block * ROWS, ROWS)
        rows = live_ref[pl.ds(first, ROWS), :]
        place = iota((TILES, ROWS), 1) + first - start
        member = ((place >= 0) & (place < live)).astype(F32).astype(BF)
        for c in range(0, D, 256):
            x = dot(rows, w_ref[:, c : c + 256]).astype(BF)
            acc_ref[:, c : c + 256] += dot(member, twice_gelu(x))

    pooled = acc_ref[...] * (0.5 / cnt[:, 0:1])
    own = jnp.broadcast_to(own_ref[...].astype(F32), square)
    own_t = own.T
    rank = jnp.sum(
        jnp.where((own == own_t) & (iota(square, 0) < iota(square, 1)), 1.0, 0.0),
        axis=0,
        keepdims=True,
    )
    slot = (2.0 * own_t[0:1, :] + rank).astype(I32)
    place = (iota((SLOTS, TILES), 0) == slot).astype(F32).astype(BF)
    cell = jnp.broadcast_to(cell_ref[...].astype(F32), square).T + 1.0
    pay_ref[:, 0:D] = dot(place, pooled.astype(BF)).astype(BF)
    pay_ref[:, D:PAY] = dot(place, cell.astype(BF)).astype(BF)


def pool_call(obs_values, tile_owner, tile_cell, tile_count, w_obs_in):
    return pl.pallas_call(
        pool_kernel,
        out_shape=jax.ShapeDtypeStruct((SLOTS, PAY), BF),
        in_specs=[SMEM] + [VMEM] * 5,
        out_specs=VMEM,
        scratch_shapes=[
            pltpu.VMEM((TILES * TROWS + ROWS, F_OBS), BF),
            pltpu.VMEM((TILES, D), F32),
        ],
        compiler_params=params(32),
        cost_estimate=cost(12),
        name="pool_tiles",
    )(
        tile_count,
        obs_values,
        tile_count.reshape(1, TILES),
        tile_owner,
        tile_cell.reshape(1, TILES),
        w_obs_in,
    )


def three(x):
    hi = x.astype(BF)
    rest = x - hi.astype(F32)
    mid = rest.astype(BF)
    lo = (rest - mid.astype(F32)).astype(BF)
    return [hi.astype(F32), mid.astype(F32), lo.astype(F32)]


def stacked(rows, count):
    place = iota((count, ROWS), 0)
    out = jnp.zeros((count, ROWS), F32)
    for i, row in enumerate(rows):
        out = jnp.where(place == i, jnp.broadcast_to(row, out.shape), out)
    return out


def value_rows(kv_ref, group):
    first = ROWS + group * HD
    return jnp.concatenate([kv_ref[first : first + HD, :], jnp.ones((VT - HD, ROWS), BF)], axis=0)


def first_kernel(rate_s, normed_ref, wq_ref, kv_ref, q_ref, out_ref, dist_ref):
    q = (dot(normed_ref[...], wq_ref[...]) * (0.125 * LOG2E)).T
    dist_ref[...] = jnp.abs(iota((ROWS, ROWS), 0) - iota((ROWS, ROWS), 1)).astype(F32)
    lane = iota((ROWS, 128), 1)
    at = iota((1, ROWS), 1).astype(F32)
    for group in range(KVH):
        even = group % 2 == 0
        pair = kv_ref[0:ROWS, (group // 2) * 128 : (group // 2) * 128 + 128]
        keys = jnp.where((lane < HD) == even, pair, jnp.zeros_like(pair))
        values = value_rows(kv_ref, group)
        for head in range(4 * group, 4 * group + 4):
            rate = rate_s[head] * LOG2E
            own = q[head * HD : head * HD + HD, :].astype(BF)
            blank = jnp.zeros((HD, ROWS), BF)
            scores = dot(keys, jnp.concatenate([own, blank] if even else [blank, own], axis=0))
            scores = scores - rate * dist_ref[...]
            top = jnp.max(scores, axis=0, keepdims=True)
            out_ref[head] = dot(values, jnp.exp2(scores - top).astype(BF))
            rates = three(jnp.full((1, ROWS), rate, F32))
            extra = stacked(
                rates + rates + three(rate * at - top) + three(-rate * at - top) + three(-top), 16
            ).astype(BF)
            extra = jnp.concatenate([extra, jnp.zeros((HD - 16, ROWS), BF)], axis=0)
            q_ref[head] = jnp.concatenate([own, extra] if even else [extra, own], axis=0)


def first_call(head_rate, normed, w_query, kv):
    return pl.pallas_call(
        first_kernel,
        out_shape=(
            jax.ShapeDtypeStruct((HEADS, 128, ROWS), BF),
            jax.ShapeDtypeStruct((HEADS, VT, ROWS), F32),
        ),
        in_specs=[SMEM] + [VMEM] * 3,
        out_specs=(VMEM, VMEM),
        scratch_shapes=[pltpu.VMEM((ROWS, ROWS), F32)],
        compiler_params=params(24),
        cost_estimate=cost(5),
        name="queries_own_rows",
    )(head_rate, normed, w_query, kv)


def place_lanes(ahead, first):
    lane = iota((ROWS, 128), 1) - first
    row = iota((ROWS, 128), 0)
    plus = jnp.where(ahead < 8, 1, 0)
    minus = jnp.where(ahead > 8, 1, 0)
    blocks = jnp.where(ahead == 8, 0, jnp.where(ahead < 8, ahead, LON - ahead))
    out = jnp.where(lane < 3, row * (minus - plus), -ROWS * blocks)
    out = jnp.where(lane < 6, out, jnp.where(lane < 9, plus, jnp.where(lane < 12, minus, 1 - plus - minus)))
    out = jnp.where((lane >= 0) & (lane < 15), out, 0)
    return out.astype(F32).astype(BF)


def other_kernel(count, half_way, chunk, ahead_s, rate_s, q_ref, part_ref, *rest):
    blocks = rest[:count]
    out_ref, key_ref, value_ref = rest[count:]
    lane = iota((ROWS, 128), 1)
    for b in range(count):
        here = pl.ds(b * ROWS, ROWS)
        extra = (place_lanes(ahead_s[b], HD), place_lanes(ahead_s[b], 0))
        for group in range(KVH):
            odd = group % 2
            pair = blocks[b][0:ROWS, (group // 2) * 128 : (group // 2) * 128 + 128]
            key_ref[group, here, :] = jnp.where((lane < HD) == (odd == 0), pair, extra[odd])
            value_ref[group, :, here] = value_rows(blocks[b], group)
    if half_way is not None:
        gap = LON // 2 * ROWS - jnp.abs(iota((ROWS, ROWS), 0) - iota((ROWS, ROWS), 1))
        gap = gap.astype(F32)

    @pl.loop(0, KVH)
    def _(group):
        for i in range(4):
            head = group * 4 + i
            total = part_ref[head]
            for first in range(0, count, chunk):
                size = min(chunk, count - first)
                here = pl.ds(first * ROWS, size * ROWS)
                scores = dot(key_ref[group, here, :], q_ref[head])
                if half_way is not None and first <= half_way < first + size:
                    at = (half_way - first) * ROWS
                    far = scores[at : at + ROWS] - (rate_s[head] * LOG2E) * gap
                    pieces = [scores[:at], far, scores[at + ROWS :]]
                    scores = jnp.concatenate([x for x in pieces if x.shape[0]], axis=0)
                total = total + dot(value_ref[group, :, here], jnp.exp2(scores).astype(BF))
            out_ref[head] = total


def other_call(ahead, head_rate, q, part, blocks, half_way, chunk, name):
    count = len(blocks)
    return pl.pallas_call(
        functools.partial(other_kernel, count, half_way, chunk),
        out_shape=jax.ShapeDtypeStruct((HEADS, VT, ROWS), F32),
        in_specs=[SMEM] * 2 + [VMEM] * (2 + count),
        out_specs=VMEM,
        scratch_shapes=[
            pltpu.VMEM((KVH, count * ROWS, 128), BF),
            pltpu.VMEM((KVH, VT, count * ROWS), BF),
        ],
        compiler_params=params(40),
        cost_estimate=cost(2 + 1.3 * count),
        name=name,
    )(ahead, head_rate, q, part, *blocks)


def careful(ahead_s, rate_s, q_ref, blocks, kvs_ref, context_ref, top_ref, sum_ref, acc_ref, sem):
    for b, block in enumerate(blocks):
        copy = pltpu.make_async_copy(block, kvs_ref.at[b], sem)
        copy.start()
        copy.wait()
    lane = iota((ROWS, 128), 1)
    for group in range(KVH):

        @pl.loop(0, 4)
        def _(i):
            head = group * 4 + i
            top_ref[...] = jnp.full((1, ROWS), -jnp.inf, F32)
            sum_ref[...] = jnp.zeros((1, ROWS), F32)
            acc_ref[...] = jnp.zeros((HD, ROWS), F32)

            @pl.loop(0, LON)
            def _(b):
                pair = kvs_ref[b, 0:ROWS, (group // 2) * 128 : (group // 2) * 128 + 128]
                keys = jnp.where((lane < HD) == (group % 2 == 0), pair, jnp.zeros_like(pair))
                gap = jnp.abs(
                    ahead_s[b] * ROWS + iota((ROWS, ROWS), 0) - iota((ROWS, ROWS), 1)
                )
                gap = jnp.minimum(gap, BAND - gap).astype(F32)
                scores = dot(keys, q_ref[head]) - (rate_s[head] * LOG2E) * gap
                top = jnp.maximum(top_ref[...], jnp.max(scores, axis=0, keepdims=True))
                shrink = jnp.exp2(top_ref[...] - top)
                weights = jnp.exp2(scores - top)
                first = ROWS + group * HD
                top_ref[...] = top
                sum_ref[...] = sum_ref[...] * shrink + jnp.sum(weights, axis=0, keepdims=True)
                acc_ref[...] = acc_ref[...] * shrink + dot(
                    kvs_ref[b, first : first + HD, :], weights.astype(BF)
                )

            context_ref[pl.ds(pl.multiple_of(head * HD, HD), HD), :] = acc_ref[...] / sum_ref[...]


STEP = 512


def last_kernel(
    ahead_s,
    rate_s,
    tok_ref,
    gain_ref,
    q_ref,
    part_ref,
    pay_ref,
    w_out_hbm,
    w_obs_hbm,
    w_up_hbm,
    w_down_hbm,
    *rest,
):
    blocks = rest[:LON]
    (
        out_ref,
        w_out_ref,
        w_obs_ref,
        w_up_ref,
        w_down_ref,
        context_ref,
        kvs_ref,
        top_ref,
        sum_ref,
        acc_ref,
        sem,
        spare,
    ) = rest[LON:]
    steps = FF // STEP
    copies = [
        pltpu.make_async_copy(w_out_hbm, w_out_ref, sem.at[0]),
        pltpu.make_async_copy(w_obs_hbm, w_obs_ref, sem.at[1]),
    ]
    for s in range(steps):
        here = pl.ds(s * STEP, STEP)
        copies.append(pltpu.make_async_copy(w_up_hbm.at[:, here], w_up_ref.at[s], sem.at[2 + 2 * s]))
        copies.append(
            pltpu.make_async_copy(w_down_hbm.at[here, :], w_down_ref.at[s], sem.at[3 + 2 * s])
        )
    for copy in copies:
        copy.start()

    largest = jnp.zeros((1, ROWS), F32)
    for head in range(HEADS):
        weight_sum = part_ref[head, HD : HD + 1, :]
        largest = jnp.maximum(largest, weight_sum)
        context_ref[head * HD : head * HD + HD, :] = part_ref[head, 0:HD, :] * (1.0 / weight_sum)

    @pl.when(jnp.logical_not(jnp.max(largest) < 2.0**100))
    def _():
        careful(
            ahead_s, rate_s, q_ref, blocks, kvs_ref, context_ref, top_ref, sum_ref, acc_ref, spare
        )

    cell = pay_ref[:, D:PAY].astype(F32).T
    cell = jnp.broadcast_to(cell[0:1, :], (ROWS, SLOTS)).astype(I32)
    place = (iota((ROWS, SLOTS), 0) + 1 == cell).astype(F32).astype(BF)
    pooled = dot(place, pay_ref[:, 0:D]).astype(BF)
    context = context_ref[...].T.astype(BF)
    copies[0].wait()
    mixed = tok_ref[...].astype(F32) + dot(context, w_out_ref[...])
    copies[1].wait()
    mixed = (mixed + dot(pooled, w_obs_ref[...])).astype(BF).astype(F32)
    normed = normed_rows(mixed, gain_ref[...])
    for s in range(steps):
        copies[2 + 2 * s].wait()
        hidden = (0.5 * twice_gelu(dot(normed, w_up_ref[s]))).astype(BF)
        copies[3 + 2 * s].wait()
        mixed = mixed + dot(hidden, w_down_ref[s])
    out_ref[...] = mixed.astype(BF)


def last_call(ahead, head_rate, tokens, gain, q, part, pay, w_out, w_obs_out, w_up, w_down, blocks):
    steps = FF // STEP
    return pl.pallas_call(
        last_kernel,
        out_shape=jax.ShapeDtypeStruct((ROWS, D), BF),
        in_specs=[SMEM] * 2 + [VMEM] * 5 + [ANY] * (4 + LON),
        out_specs=VMEM,
        scratch_shapes=[
            pltpu.VMEM((D, D), BF),
            pltpu.VMEM((D, D), BF),
            pltpu.VMEM((steps, D, STEP), BF),
            pltpu.VMEM((steps, STEP, D), BF),
            pltpu.VMEM((D, ROWS), F32),
            pltpu.VMEM((LON, 2 * ROWS, KVH * HD), BF),
            pltpu.VMEM((1, ROWS), F32),
            pltpu.VMEM((1, ROWS), F32),
            pltpu.VMEM((HD, ROWS), F32),
            pltpu.SemaphoreType.DMA((2 + 2 * steps,)),
            pltpu.SemaphoreType.DMA,
        ],
        compiler_params=params(48),
        cost_estimate=cost(9),
        name="project_update_mlp",
    )(
        ahead,
        head_rate,
        tokens,
        gain.reshape(1, D),
        q,
        part,
        pay,
        w_out,
        w_obs_out,
        w_up,
        w_down,
        *blocks,
    )


def lon_of(x, z, core):
    return x * 8 + (z % 4) * 2 + core


def send(block, flip_x, step_z, flip_core):
    pairs = [
        (lon_of(x, z, core), lon_of(x ^ flip_x, z + step_z, core ^ flip_core))
        for x in range(2)
        for z in range(4)
        for core in range(2)
    ]
    return lax.ppermute(block, "lon", pairs)


def ahead_of(moves):
    me = lax.axis_index("lon")
    x, z, core = me // 8, (me // 2) % 4, me % 2
    sources = [
        lax.rem(x + fx, 2) * 8 + lax.rem(z + 4 - dz, 4) * 2 + lax.rem(core + fc, 2)
        for fx, dz, fc in moves
    ]
    return jnp.stack([lax.rem(s - me + LON, LON) for s in sources]).astype(I32)


def shards(
    tokens,
    attn_gain,
    w_query,
    w_key,
    w_value,
    w_out,
    head_rate,
    obs_values,
    tile_owner,
    tile_cell,
    tile_count,
    w_obs_in,
    w_obs_out,
    mlp_gain,
    w_up,
    w_down,
):
    normed, kv = kv_call(tokens, attn_gain, w_key, w_value)
    up = send(kv, 0, 1, 0)
    down = send(kv, 0, 3, 0)
    across = send(kv, 1, 0, 0)
    far = send(kv, 0, 2, 0)
    sibling = send(kv, 0, 0, 1)
    pay = pool_call(obs_values, tile_owner, tile_cell, tile_count, w_obs_in)
    pay = lax.all_to_all(pay, ("lat", "lon"), split_axis=0, concat_axis=0, tiled=True)
    q, part = first_call(head_rate, normed, w_query, kv)

    near = [across, up, down, far]
    near_moves = [(1, 0, 0), (0, 1, 0), (0, 3, 0), (0, 2, 0)]
    late = [send(across, 0, 1, 0), send(across, 0, 3, 0), send(far, 1, 0, 0)]
    late_moves = [(1, 1, 0), (1, 3, 0), (1, 2, 0)]
    flip = lambda moves: [(x, z, 1) for x, z, _ in moves]
    near_twin = [send(b, 0, 0, 1) for b in near]
    late_twin = [send(b, 0, 0, 1) for b in late]

    stage_one = near + [sibling] + near_twin
    stage_two = late + late_twin
    moves_one = near_moves + [(0, 0, 1)] + flip(near_moves)
    moves_two = late_moves + flip(late_moves)
    part = other_call(
        ahead_of(moves_one), head_rate, q, part, stage_one, 0, 3, "near_rows"
    )
    part = other_call(
        ahead_of(moves_two), head_rate, q, part, stage_two, None, 3, "late_rows"
    )
    return last_call(
        ahead_of([(0, 0, 0)] + moves_one + moves_two),
        head_rate,
        tokens,
        mlp_gain,
        q,
        part,
        pay,
        w_out,
        w_obs_out,
        w_up,
        w_down,
        [kv] + stage_one + stage_two,
    )


def solution(mesh):
    shard = P(("lat", "lon"))
    rows = P(("lat", "lon"), None)
    return jax.shard_map(
        shards,
        mesh=mesh,
        in_specs=(rows,)
        + (P(),) * 6
        + (P(("lat", "lon"), None, None), rows, shard, shard)
        + (P(),) * 5,
        out_specs=rows,
        check_vma=False,
    )
```

```python
import functools
import math

import jax
import jax.numpy as jnp
from jax import lax
from jax.experimental import pallas as pl
from jax.experimental.pallas import tpu as pltpu
from jax.sharding import PartitionSpec as P

BF = jnp.bfloat16
F32 = jnp.float32
I32 = jnp.int32

D = 1024
HEADS = 16
HD = 64
KVH = 4
FF = 4096
ROWS = 256
TILES = 128
TROWS = 128
F_OBS = 32
LON = 16
BAND = ROWS * LON
SLOTS = 256
PAY = D + 128
LOG2E = 1.4426950408889634
VT = HD + 16
MIB = 2**20
VMEM = pl.BlockSpec(memory_space=pltpu.VMEM)
SMEM = pl.BlockSpec(memory_space=pltpu.SMEM)
ANY = pl.BlockSpec(memory_space=pl.ANY)


def iota(shape, dim):
    return lax.broadcasted_iota(I32, shape, dim)


def params(mib):
    return pltpu.CompilerParams(vmem_limit_bytes=mib * MIB)


def cost(micros):
    return pl.CostEstimate(
        flops=int(micros * 1.0e9), bytes_accessed=int(micros * 1.0e6), transcendentals=0
    )


def dot(a, b):
    return jnp.dot(a, b, preferred_element_type=F32)


def normed_rows(rows, gain):
    mean_square = jnp.mean(rows * rows, axis=-1, keepdims=True)
    return (rows * lax.rsqrt(mean_square + 1e-05) * gain).astype(BF)


def twice_gelu(x):
    k0 = math.sqrt(2.0 / math.pi)
    k1 = k0 * 0.044715
    inner = x * (x * x * k1 + k0)
    return jnp.tanh(inner) * x + x


def kv_kernel(tok_ref, gain_ref, wk_ref, wv_ref, normed_ref, kv_ref):
    normed = normed_rows(tok_ref[...].astype(F32), gain_ref[...])
    normed_ref[...] = normed
    kv_ref[0:ROWS, :] = dot(normed, wk_ref[...]).astype(BF)
    kv_ref[ROWS : 2 * ROWS, :] = dot(normed, wv_ref[...]).T.astype(BF)


def kv_call(tokens, gain, w_key, w_value):
    return pl.pallas_call(
        kv_kernel,
        out_shape=(
            jax.ShapeDtypeStruct((ROWS, D), BF),
            jax.ShapeDtypeStruct((2 * ROWS, KVH * HD), BF),
        ),
        in_specs=[VMEM] * 4,
        out_specs=(VMEM, VMEM),
        compiler_params=params(60),
        cost_estimate=cost(3),
        name="norm_keys_values",
    )(tokens, gain.reshape(1, D), w_key, w_value)


BLOCK = 512
HALF = BLOCK // 2
COLS = 512


def pool_kernel(
    cnt_s, obs_ref, cnt_ref, own_ref, cell_ref, w_ref, pay_ref, live_ref, acc_ref, act_ref, member_ref
):
    square = (TILES, TILES)
    source = iota(square, 1) // F_OBS
    row = iota(square, 0)

    def put(step, first):
        for u in range(2):
            four = step * 2 + u
            rows = obs_ref[pl.ds(pl.multiple_of(four * TILES, TILES), TILES), :].T
            for k in range(4):
                count = cnt_s[four * 4 + k]
                live_ref[pl.ds(pl.multiple_of(first, 32), TROWS), :] = jnp.where(
                    (source == k) & (row < count), rows, jnp.zeros_like(rows)
                )
                first = first + ((count + 31) // 32) * 32
        return first

    total = lax.fori_loop(0, TILES // 8, put, jnp.int32(0))
    for i in range(0, 2 * BLOCK, 128):
        live_ref[pl.ds(pl.multiple_of(total + i, 32), 128), :] = jnp.zeros(square, BF)

    weights = jnp.concatenate([w_ref[...]] * 4, axis=0)
    cnt = jnp.broadcast_to(cnt_ref[...].astype(F32), square).T
    groups = jnp.floor((cnt + 31.0) * (1.0 / 32.0))
    earlier = (iota(square, 1) < iota(square, 0)).astype(F32)
    start = dot(earlier.astype(BF), groups.astype(BF)) * 16.0
    start = jnp.concatenate([start] * (HALF // 128), axis=1)
    length = jnp.concatenate([groups * 16.0] * (HALF // 128), axis=1)

    acc_ref[...] = jnp.zeros_like(acc_ref)
    act_ref[...] = jnp.zeros_like(act_ref)
    member_ref[...] = jnp.zeros_like(member_ref)

    def one_block(block, now):
        old = 1 - now
        rows = live_ref[pl.ds(pl.multiple_of(block * BLOCK, BLOCK), BLOCK), :]
        place = (iota((TILES, HALF), 1) + block * HALF).astype(F32) - start
        member_ref[now] = ((place >= 0) & (place < length)).astype(F32).astype(BF)
        for c in range(0, D, COLS):
            here = slice(c, c + COLS)
            x = dot(rows, weights[:, here])
            acc_ref[:, here] += dot(member_ref[old], act_ref[old, :, here])
            act = twice_gelu(x.astype(BF))
            act_ref[now, :, here] = jnp.concatenate(
                [act[i : i + 16] + act[i + 16 : i + 32] for i in range(0, BLOCK, 32)], axis=0
            )

    @pl.loop(0, (total + 2 * BLOCK - 1) // (2 * BLOCK))
    def _(pair):
        one_block(2 * pair, 0)
        one_block(2 * pair + 1, 1)

    pooled = (acc_ref[...] + dot(member_ref[1], act_ref[1])) * (0.5 / cnt[:, 0:1])
    own_t = jnp.broadcast_to(own_ref[...].astype(F32), square)
    rank = jnp.sum(
        jnp.where((own_t.T == own_t) & (iota(square, 0) < iota(square, 1)), 1.0, 0.0),
        axis=0,
        keepdims=True,
    )
    slot = (2.0 * own_t[0:1, :] + rank).astype(I32)
    place = (iota((SLOTS, TILES), 0) == slot).astype(F32).astype(BF)
    cell = jnp.broadcast_to(cell_ref[...].astype(F32), square).T + 1.0
    pay_ref[:, 0:D] = dot(place, pooled.astype(BF)).astype(BF)
    pay_ref[:, D:PAY] = dot(place, cell.astype(BF)).astype(BF)


def pool_call(obs_values, tile_owner, tile_cell, tile_count, w_obs_in):
    return pl.pallas_call(
        pool_kernel,
        out_shape=jax.ShapeDtypeStruct((SLOTS, PAY), BF),
        in_specs=[SMEM] + [VMEM] * 5,
        out_specs=VMEM,
        scratch_shapes=[
            pltpu.VMEM((TILES * TROWS + 2 * BLOCK, 128), BF),
            pltpu.VMEM((TILES, D), F32),
            pltpu.VMEM((2, HALF, D), BF),
            pltpu.VMEM((2, TILES, HALF), BF),
        ],
        compiler_params=params(60),
        cost_estimate=cost(15),
        name="pool_tiles",
    )(
        tile_count,
        jnp.transpose(obs_values, (0, 2, 1)).reshape(TILES * F_OBS, TROWS),
        tile_count.reshape(1, TILES),
        tile_owner.reshape(1, TILES),
        tile_cell.reshape(1, TILES),
        w_obs_in,
    )


def three(x):
    hi = x.astype(BF)
    rest = x - hi.astype(F32)
    mid = rest.astype(BF)
    lo = (rest - mid.astype(F32)).astype(BF)
    return [hi.astype(F32), mid.astype(F32), lo.astype(F32)]


def stacked(rows, count):
    place = iota((count, ROWS), 0)
    out = jnp.zeros((count, ROWS), F32)
    for i, row in enumerate(rows):
        out = jnp.where(place == i, jnp.broadcast_to(row, out.shape), out)
    return out


def value_rows(kv_ref, group):
    first = ROWS + group * HD
    return jnp.concatenate([kv_ref[first : first + HD, :], jnp.ones((VT - HD, ROWS), BF)], axis=0)


def first_kernel(rate_s, normed_ref, wq_ref, kv_ref, q_ref, out_ref, dist_ref):
    q = (dot(normed_ref[...], wq_ref[...]) * (0.125 * LOG2E)).T
    dist_ref[...] = jnp.abs(iota((ROWS, ROWS), 0) - iota((ROWS, ROWS), 1)).astype(F32)
    lane = iota((ROWS, 128), 1)
    at = iota((1, ROWS), 1).astype(F32)
    for group in range(KVH):
        even = group % 2 == 0
        pair = kv_ref[0:ROWS, (group // 2) * 128 : (group // 2) * 128 + 128]
        keys = jnp.where((lane < HD) == even, pair, jnp.zeros_like(pair))
        values = value_rows(kv_ref, group)
        for head in range(4 * group, 4 * group + 4):
            rate = rate_s[head] * LOG2E
            own = q[head * HD : head * HD + HD, :].astype(BF)
            blank = jnp.zeros((HD, ROWS), BF)
            scores = dot(keys, jnp.concatenate([own, blank] if even else [blank, own], axis=0))
            scores = scores - rate * dist_ref[...]
            top = jnp.max(scores, axis=0, keepdims=True)
            out_ref[head] = dot(values, jnp.exp2(scores - top).astype(BF))
            rates = three(jnp.full((1, ROWS), rate, F32))
            extra = stacked(
                rates + rates + three(rate * at - top) + three(-rate * at - top) + three(-top), 16
            ).astype(BF)
            extra = jnp.concatenate([extra, jnp.zeros((HD - 16, ROWS), BF)], axis=0)
            q_ref[head] = jnp.concatenate([own, extra] if even else [extra, own], axis=0)


def first_call(head_rate, normed, w_query, kv):
    return pl.pallas_call(
        first_kernel,
        out_shape=(
            jax.ShapeDtypeStruct((HEADS, 128, ROWS), BF),
            jax.ShapeDtypeStruct((HEADS, VT, ROWS), F32),
        ),
        in_specs=[SMEM] + [VMEM] * 3,
        out_specs=(VMEM, VMEM),
        scratch_shapes=[pltpu.VMEM((ROWS, ROWS), F32)],
        compiler_params=params(60),
        cost_estimate=cost(5),
        name="queries_own_rows",
    )(head_rate, normed, w_query, kv)


def place_lanes(ahead, first):
    lane = iota((ROWS, 128), 1) - first
    row = iota((ROWS, 128), 0)
    plus = jnp.where(ahead < 8, 1, 0)
    minus = jnp.where(ahead > 8, 1, 0)
    blocks = jnp.where(ahead == 8, 0, jnp.where(ahead < 8, ahead, LON - ahead))
    out = jnp.where(lane < 3, row * (minus - plus), -ROWS * blocks)
    out = jnp.where(lane < 6, out, jnp.where(lane < 9, plus, jnp.where(lane < 12, minus, 1 - plus - minus)))
    out = jnp.where((lane >= 0) & (lane < 15), out, 0)
    return out.astype(F32).astype(BF)


def careful(ahead, rate_s, q_ref, key_ref, value_ref, ahead_ref, context_ref, top_ref, sum_ref, acc_ref):
    for b in range(LON):
        ahead_ref[b] = ahead[b]
    lane = iota((ROWS, 128), 1)
    for group in range(KVH):

        @pl.loop(0, 4)
        def _(i):
            head = group * 4 + i
            top_ref[...] = jnp.full((1, ROWS), -jnp.inf, F32)
            sum_ref[...] = jnp.zeros((1, ROWS), F32)
            acc_ref[...] = jnp.zeros((HD, ROWS), F32)

            @pl.loop(0, LON)
            def _(b):
                here = pl.ds(pl.multiple_of(b * ROWS, ROWS), ROWS)
                keys = key_ref[group, here, :]
                keys = jnp.where((lane < HD) == (group % 2 == 0), keys, jnp.zeros_like(keys))
                gap = jnp.abs(ahead_ref[b] * ROWS + iota((ROWS, ROWS), 0) - iota((ROWS, ROWS), 1))
                gap = jnp.minimum(gap, BAND - gap).astype(F32)
                scores = dot(keys, q_ref[head]) - (rate_s[head] * LOG2E) * gap
                top = jnp.maximum(top_ref[...], jnp.max(scores, axis=0, keepdims=True))
                shrink = jnp.exp2(top_ref[...] - top)
                weights = jnp.exp2(scores - top)
                top_ref[...] = top
                sum_ref[...] = sum_ref[...] * shrink + jnp.sum(weights, axis=0, keepdims=True)
                acc_ref[...] = acc_ref[...] * shrink + dot(
                    value_ref[group, 0:HD, here], weights.astype(BF)
                )

            context_ref[pl.ds(pl.multiple_of(head * HD, HD), HD), :] = acc_ref[...] / sum_ref[...]


STEP = 1024
STEPS = FF // STEP
CHUNK = 5


def last_kernel(
    moves,
    rate_s,
    tok_ref,
    gain_ref,
    q_ref,
    part_ref,
    pay_ref,
    w_out_hbm,
    w_obs_hbm,
    w_up_hbm,
    w_down_hbm,
    *rest,
):
    blocks = rest[:LON]
    (
        out_ref,
        w_out_ref,
        w_obs_ref,
        w_up_ref,
        w_down_ref,
        key_ref,
        value_ref,
        context_ref,
        largest_ref,
        ahead_ref,
        top_ref,
        sum_ref,
        acc_ref,
        sem,
    ) = rest[LON:]
    copies = [
        pltpu.make_async_copy(w_out_hbm, w_out_ref, sem.at[0]),
        pltpu.make_async_copy(w_obs_hbm, w_obs_ref, sem.at[1]),
    ]
    for s in range(STEPS):
        here = pl.ds(s * STEP, STEP)
        copies.append(pltpu.make_async_copy(w_up_hbm.at[:, here], w_up_ref.at[s], sem.at[2 + 2 * s]))
        copies.append(
            pltpu.make_async_copy(w_down_hbm.at[here, :], w_down_ref.at[s], sem.at[3 + 2 * s])
        )
    for copy in copies:
        copy.start()

    ahead = ahead_of(moves)
    lane = iota((ROWS, 128), 1)
    for b in range(LON):
        here = pl.ds(b * ROWS, ROWS)
        extra = (place_lanes(ahead[b], HD), place_lanes(ahead[b], 0))
        for group in range(KVH):
            odd = group % 2
            pair = blocks[b][0:ROWS, (group // 2) * 128 : (group // 2) * 128 + 128]
            key_ref[group, here, :] = jnp.where((lane < HD) == (odd == 0), pair, extra[odd])
            value_ref[group, :, here] = value_rows(blocks[b], group)
    gap = LON // 2 * ROWS - jnp.abs(iota((ROWS, ROWS), 0) - iota((ROWS, ROWS), 1))
    gap = gap.astype(F32)
    largest_ref[...] = jnp.zeros((1, ROWS), F32)

    @pl.loop(0, KVH)
    def _(group):
        for i in range(4):
            head = group * 4 + i
            total = part_ref[head]
            for first in range(1, LON, CHUNK):
                here = pl.ds(first * ROWS, CHUNK * ROWS)
                scores = dot(key_ref[group, here, :], q_ref[head])
                if first == 1:
                    far = scores[:ROWS] - (rate_s[head] * LOG2E) * gap
                    scores = jnp.concatenate([far, scores[ROWS:]], axis=0)
                total = total + dot(value_ref[group, :, here], jnp.exp2(scores).astype(BF))
            weight_sum = total[HD : HD + 1]
            largest_ref[...] = jnp.maximum(largest_ref[...], weight_sum)
            context_ref[pl.ds(pl.multiple_of(head * HD, HD), HD), :] = total[:HD] * (
                1.0 / weight_sum
            )

    @pl.when(jnp.logical_not(jnp.max(largest_ref[...]) < 2.0**100))
    def _():
        careful(
            ahead, rate_s, q_ref, key_ref, value_ref, ahead_ref, context_ref, top_ref, sum_ref, acc_ref
        )

    cell = pay_ref[:, D:PAY].astype(F32).T
    cell = jnp.broadcast_to(cell[0:1, :], (ROWS, SLOTS)).astype(I32)
    place = (iota((ROWS, SLOTS), 0) + 1 == cell).astype(F32).astype(BF)
    pooled = dot(place, pay_ref[:, 0:D]).astype(BF)
    context = context_ref[...].T.astype(BF)
    copies[0].wait()
    mixed = tok_ref[...].astype(F32) + dot(context, w_out_ref[...])
    copies[1].wait()
    mixed = (mixed + dot(pooled, w_obs_ref[...])).astype(BF).astype(F32)
    normed = normed_rows(mixed, gain_ref[...])
    for s in range(STEPS):
        copies[2 + 2 * s].wait()
        hidden = (0.5 * twice_gelu(dot(normed, w_up_ref[s]))).astype(BF)
        copies[3 + 2 * s].wait()
        mixed = mixed + dot(hidden, w_down_ref[s])
    out_ref[...] = mixed.astype(BF)


def last_call(moves, head_rate, tokens, gain, q, part, pay, w_out, w_obs_out, w_up, w_down, blocks):
    return pl.pallas_call(
        functools.partial(last_kernel, moves),
        out_shape=jax.ShapeDtypeStruct((ROWS, D), BF),
        in_specs=[SMEM] + [VMEM] * 5 + [ANY] * 4 + [VMEM] * LON,
        out_specs=VMEM,
        scratch_shapes=[
            pltpu.VMEM((D, D), BF),
            pltpu.VMEM((D, D), BF),
            pltpu.VMEM((STEPS, D, STEP), BF),
            pltpu.VMEM((STEPS, STEP, D), BF),
            pltpu.VMEM((KVH, BAND, 128), BF),
            pltpu.VMEM((KVH, VT, BAND), BF),
            pltpu.VMEM((D, ROWS), F32),
            pltpu.VMEM((1, ROWS), F32),
            pltpu.SMEM((LON,), I32),
            pltpu.VMEM((1, ROWS), F32),
            pltpu.VMEM((1, ROWS), F32),
            pltpu.VMEM((HD, ROWS), F32),
            pltpu.SemaphoreType.DMA((2 + 2 * STEPS,)),
        ],
        compiler_params=params(60),
        cost_estimate=cost(24),
        name="other_rows_project_update_mlp",
    )(
        head_rate,
        tokens,
        gain.reshape(1, D),
        q,
        part,
        pay,
        w_out,
        w_obs_out,
        w_up,
        w_down,
        *blocks,
    )


def lon_of(x, z, core):
    return x * 8 + (z % 4) * 2 + core


def send(block, flip_x, step_z, flip_core):
    pairs = [
        (lon_of(x, z, core), lon_of(x ^ flip_x, z + step_z, core ^ flip_core))
        for x in range(2)
        for z in range(4)
        for core in range(2)
    ]
    return lax.ppermute(block, "lon", pairs)


def ahead_of(moves):
    me = lax.axis_index("lon")
    x, z, core = me // 8, (me // 2) % 4, me % 2
    sources = [
        lax.rem(x + fx, 2) * 8 + lax.rem(z + 4 - dz, 4) * 2 + lax.rem(core + fc, 2)
        for fx, dz, fc in moves
    ]
    return [lax.rem(s - me + LON, LON) for s in sources]


def shards(
    tokens,
    attn_gain,
    w_query,
    w_key,
    w_value,
    w_out,
    head_rate,
    obs_values,
    tile_owner,
    tile_cell,
    tile_count,
    w_obs_in,
    w_obs_out,
    mlp_gain,
    w_up,
    w_down,
):
    normed, kv = kv_call(tokens, attn_gain, w_key, w_value)
    up = send(kv, 0, 1, 0)
    down = send(kv, 0, 3, 0)
    across = send(kv, 1, 0, 0)
    far = send(kv, 0, 2, 0)
    sibling = send(kv, 0, 0, 1)
    q, part = first_call(head_rate, normed, w_query, kv)
    part, tile_count, up, down, across, far, sibling = lax.optimization_barrier(
        (part, tile_count, up, down, across, far, sibling)
    )
    late = [send(across, 0, 1, 0), send(across, 0, 3, 0), send(far, 1, 0, 0)]
    near = [across, up, down, far]
    near_twin = [send(b, 0, 0, 1) for b in near]
    pay = pool_call(obs_values, tile_owner, tile_cell, tile_count, w_obs_in)
    pay, *late = lax.optimization_barrier((pay, *late, *near_twin))
    late, near_twin = late[:3], late[3:]
    late_twin = [send(b, 0, 0, 1) for b in late]
    pay = lax.all_to_all(pay, ("lat", "lon"), split_axis=0, concat_axis=0, tiled=True)

    near_moves = [(1, 0, 0), (0, 1, 0), (0, 3, 0), (0, 2, 0)]
    late_moves = [(1, 1, 0), (1, 3, 0), (1, 2, 0)]
    moves = [(0, 0, 0)] + near_moves + late_moves + [(0, 0, 1)]
    moves = moves + [(x, z, 1) for x, z, _ in near_moves + late_moves]
    return last_call(
        moves,
        head_rate,
        tokens,
        mlp_gain,
        q,
        part,
        pay,
        w_out,
        w_obs_out,
        w_up,
        w_down,
        [kv] + near + late + [sibling] + near_twin + late_twin,
    )


def solution(mesh):
    shard = P(("lat", "lon"))
    rows = P(("lat", "lon"), None)
    return jax.shard_map(
        shards,
        mesh=mesh,
        in_specs=(rows,)
        + (P(),) * 6
        + (P(("lat", "lon"), None, None), rows, shard, shard)
        + (P(),) * 5,
        out_specs=rows,
        check_vma=False,
    )
```

```python
import functools
import math

import jax
import jax.numpy as jnp
from jax import lax
from jax.experimental import pallas as pl
from jax.experimental.pallas import tpu as pltpu
from jax.sharding import PartitionSpec as P

BF = jnp.bfloat16
F32 = jnp.float32
I32 = jnp.int32

D = 1024
HEADS = 16
HD = 64
KVH = 4
FF = 4096
ROWS = 256
TILES = 128
TROWS = 128
F_OBS = 32
LON = 16
BAND = ROWS * LON
SLOTS = 256
PAY = D + 128
LOG2E = 1.4426950408889634
VT = HD + 16
MIB = 2**20
VMEM = pl.BlockSpec(memory_space=pltpu.VMEM)
SMEM = pl.BlockSpec(memory_space=pltpu.SMEM)
ANY = pl.BlockSpec(memory_space=pl.ANY)


def iota(shape, dim):
    return lax.broadcasted_iota(I32, shape, dim)


def params(mib):
    return pltpu.CompilerParams(vmem_limit_bytes=mib * MIB)


def cost(micros):
    return pl.CostEstimate(
        flops=int(micros * 1.0e9), bytes_accessed=int(micros * 1.0e6), transcendentals=0
    )


def dot(a, b):
    return jnp.dot(a, b, preferred_element_type=F32)


def normed_rows(rows, gain):
    mean_square = jnp.mean(rows * rows, axis=-1, keepdims=True)
    return (rows * lax.rsqrt(mean_square + 1e-05) * gain).astype(BF)


def twice_gelu(x):
    k0 = math.sqrt(2.0 / math.pi)
    k1 = k0 * 0.044715
    inner = x * (x * x * k1 + k0)
    return jnp.tanh(inner) * x + x


def kv_kernel(tok_ref, gain_ref, wk_ref, wv_ref, normed_ref, kv_ref):
    normed = normed_rows(tok_ref[...].astype(F32), gain_ref[...])
    normed_ref[...] = normed
    kv_ref[0:ROWS, :] = dot(normed, wk_ref[...]).astype(BF)
    kv_ref[ROWS : 2 * ROWS, :] = dot(normed, wv_ref[...]).T.astype(BF)


def kv_call(tokens, gain, w_key, w_value):
    return pl.pallas_call(
        kv_kernel,
        out_shape=(
            jax.ShapeDtypeStruct((ROWS, D), BF),
            jax.ShapeDtypeStruct((2 * ROWS, KVH * HD), BF),
        ),
        in_specs=[VMEM] * 4,
        out_specs=(VMEM, VMEM),
        compiler_params=params(60),
        cost_estimate=cost(3),
        name="norm_keys_values",
    )(tokens, gain.reshape(1, D), w_key, w_value)


BLOCK = 512
HALF = BLOCK // 2
COLS = 512


def pool_kernel(
    cnt_s, obs_ref, cnt_ref, own_ref, cell_ref, w_ref, pay_ref, live_ref, acc_ref, act_ref, member_ref
):
    square = (TILES, TILES)
    source = iota(square, 1) // F_OBS
    row = iota(square, 0)

    def put(step, first):
        for u in range(2):
            four = step * 2 + u
            rows = obs_ref[pl.ds(pl.multiple_of(four * TILES, TILES), TILES), :].T
            for k in range(4):
                count = cnt_s[four * 4 + k]
                live_ref[pl.ds(pl.multiple_of(first, 32), TROWS), :] = jnp.where(
                    (source == k) & (row < count), rows, jnp.zeros_like(rows)
                )
                first = first + ((count + 31) // 32) * 32
        return first

    total = lax.fori_loop(0, TILES // 8, put, jnp.int32(0))
    for i in range(0, 2 * BLOCK, 128):
        live_ref[pl.ds(pl.multiple_of(total + i, 32), 128), :] = jnp.zeros(square, BF)

    weights = jnp.concatenate([w_ref[...]] * 4, axis=0)
    cnt = jnp.broadcast_to(cnt_ref[...].astype(F32), square).T
    groups = jnp.floor((cnt + 31.0) * (1.0 / 32.0))
    earlier = (iota(square, 1) < iota(square, 0)).astype(F32)
    start = dot(earlier.astype(BF), groups.astype(BF)) * 16.0
    start = jnp.concatenate([start] * (HALF // 128), axis=1)
    length = jnp.concatenate([groups * 16.0] * (HALF // 128), axis=1)

    acc_ref[...] = jnp.zeros_like(acc_ref)
    act_ref[...] = jnp.zeros_like(act_ref)
    member_ref[...] = jnp.zeros_like(member_ref)

    def one_block(block, now):
        old = 1 - now
        rows = live_ref[pl.ds(pl.multiple_of(block * BLOCK, BLOCK), BLOCK), :]
        place = (iota((TILES, HALF), 1) + block * HALF).astype(F32) - start
        member_ref[now] = ((place >= 0) & (place < length)).astype(F32).astype(BF)
        for c in range(0, D, COLS):
            here = slice(c, c + COLS)
            x = dot(rows, weights[:, here])
            acc_ref[:, here] += dot(member_ref[old], act_ref[old, :, here])
            act = twice_gelu(x.astype(BF))
            act_ref[now, :, here] = jnp.concatenate(
                [act[i : i + 16] + act[i + 16 : i + 32] for i in range(0, BLOCK, 32)], axis=0
            )

    @pl.loop(0, (total + 2 * BLOCK - 1) // (2 * BLOCK))
    def _(pair):
        one_block(2 * pair, 0)
        one_block(2 * pair + 1, 1)

    pooled = (acc_ref[...] + dot(member_ref[1], act_ref[1])) * (0.5 / cnt[:, 0:1])
    own_t = jnp.broadcast_to(own_ref[...].astype(F32), square)
    rank = jnp.sum(
        jnp.where((own_t.T == own_t) & (iota(square, 0) < iota(square, 1)), 1.0, 0.0),
        axis=0,
        keepdims=True,
    )
    slot = (2.0 * own_t[0:1, :] + rank).astype(I32)
    cell = (jnp.broadcast_to(cell_ref[...].astype(F32), square).T + 1.0).astype(BF)
    for k in range(2):
        place = (2 * iota(square, 0) + k == slot).astype(F32).astype(BF)
        pay_ref[:, k, 0:D] = dot(place, pooled.astype(BF)).astype(BF)
        pay_ref[:, k, D:PAY] = dot(place, cell).astype(BF)


def pool_call(obs_values, tile_owner, tile_cell, tile_count, w_obs_in):
    return pl.pallas_call(
        pool_kernel,
        out_shape=jax.ShapeDtypeStruct((SLOTS // 2, 2, PAY), BF),
        in_specs=[SMEM] + [VMEM] * 5,
        out_specs=VMEM,
        scratch_shapes=[
            pltpu.VMEM((TILES * TROWS + 2 * BLOCK, 128), BF),
            pltpu.VMEM((TILES, D), F32),
            pltpu.VMEM((2, HALF, D), BF),
            pltpu.VMEM((2, TILES, HALF), BF),
        ],
        compiler_params=params(60),
        cost_estimate=cost(15),
        name="pool_tiles",
    )(
        tile_count,
        jnp.transpose(obs_values, (0, 2, 1)).reshape(TILES * F_OBS, TROWS),
        tile_count.reshape(1, TILES),
        tile_owner.reshape(1, TILES),
        tile_cell.reshape(1, TILES),
        w_obs_in,
    )


def three(x):
    hi = x.astype(BF)
    rest = x - hi.astype(F32)
    mid = rest.astype(BF)
    lo = (rest - mid.astype(F32)).astype(BF)
    return [hi.astype(F32), mid.astype(F32), lo.astype(F32)]


def stacked(rows, count):
    place = iota((count, ROWS), 0)
    out = jnp.zeros((count, ROWS), F32)
    for i, row in enumerate(rows):
        out = jnp.where(place == i, jnp.broadcast_to(row, out.shape), out)
    return out


def value_rows(kv_ref, group):
    first = ROWS + group * HD
    return jnp.concatenate([kv_ref[first : first + HD, :], jnp.ones((VT - HD, ROWS), BF)], axis=0)


def first_kernel(rate_s, normed_ref, wq_ref, kv_ref, q_ref, out_ref, dist_ref):
    q = (dot(normed_ref[...], wq_ref[...]) * (0.125 * LOG2E)).T
    dist_ref[...] = jnp.abs(iota((ROWS, ROWS), 0) - iota((ROWS, ROWS), 1)).astype(F32)
    lane = iota((ROWS, 128), 1)
    at = iota((1, ROWS), 1).astype(F32)
    for group in range(KVH):
        even = group % 2 == 0
        pair = kv_ref[0:ROWS, (group // 2) * 128 : (group // 2) * 128 + 128]
        keys = jnp.where((lane < HD) == even, pair, jnp.zeros_like(pair))
        values = value_rows(kv_ref, group)
        for head in range(4 * group, 4 * group + 4):
            rate = rate_s[head] * LOG2E
            own = q[head * HD : head * HD + HD, :].astype(BF)
            blank = jnp.zeros((HD, ROWS), BF)
            scores = dot(keys, jnp.concatenate([own, blank] if even else [blank, own], axis=0))
            scores = scores - rate * dist_ref[...]
            top = jnp.max(scores, axis=0, keepdims=True)
            out_ref[head] = dot(values, jnp.exp2(scores - top).astype(BF))
            rates = three(jnp.full((1, ROWS), rate, F32))
            extra = stacked(
                rates + rates + three(rate * at - top) + three(-rate * at - top) + three(-top), 16
            ).astype(BF)
            extra = jnp.concatenate([extra, jnp.zeros((HD - 16, ROWS), BF)], axis=0)
            q_ref[head] = jnp.concatenate([own, extra] if even else [extra, own], axis=0)


def first_call(head_rate, normed, w_query, kv):
    return pl.pallas_call(
        first_kernel,
        out_shape=(
            jax.ShapeDtypeStruct((HEADS, 128, ROWS), BF),
            jax.ShapeDtypeStruct((HEADS, VT, ROWS), F32),
        ),
        in_specs=[SMEM] + [VMEM] * 3,
        out_specs=(VMEM, VMEM),
        scratch_shapes=[pltpu.VMEM((ROWS, ROWS), F32)],
        compiler_params=params(60),
        cost_estimate=cost(5),
        name="queries_own_rows",
    )(head_rate, normed, w_query, kv)


def place_lanes(ahead, first):
    lane = iota((ROWS, 128), 1) - first
    row = iota((ROWS, 128), 0)
    plus = jnp.where(ahead < 8, 1, 0)
    minus = jnp.where(ahead > 8, 1, 0)
    blocks = jnp.where(ahead == 8, 0, jnp.where(ahead < 8, ahead, LON - ahead))
    out = jnp.where(lane < 3, row * (minus - plus), -ROWS * blocks)
    out = jnp.where(lane < 6, out, jnp.where(lane < 9, plus, jnp.where(lane < 12, minus, 1 - plus - minus)))
    out = jnp.where((lane >= 0) & (lane < 15), out, 0)
    return out.astype(F32).astype(BF)


def careful(ahead, rate_s, q_ref, key_ref, value_ref, ahead_ref, context_ref, top_ref, sum_ref, acc_ref):
    for b in range(LON):
        ahead_ref[b] = ahead[b]
    lane = iota((ROWS, 128), 1)
    for group in range(KVH):

        @pl.loop(0, 4)
        def _(i):
            head = group * 4 + i
            top_ref[...] = jnp.full((1, ROWS), -jnp.inf, F32)
            sum_ref[...] = jnp.zeros((1, ROWS), F32)
            acc_ref[...] = jnp.zeros((HD, ROWS), F32)

            @pl.loop(0, LON)
            def _(b):
                here = pl.ds(pl.multiple_of(b * ROWS, ROWS), ROWS)
                keys = key_ref[group, here, :]
                keys = jnp.where((lane < HD) == (group % 2 == 0), keys, jnp.zeros_like(keys))
                gap = jnp.abs(ahead_ref[b] * ROWS + iota((ROWS, ROWS), 0) - iota((ROWS, ROWS), 1))
                gap = jnp.minimum(gap, BAND - gap).astype(F32)
                scores = dot(keys, q_ref[head]) - (rate_s[head] * LOG2E) * gap
                top = jnp.maximum(top_ref[...], jnp.max(scores, axis=0, keepdims=True))
                shrink = jnp.exp2(top_ref[...] - top)
                weights = jnp.exp2(scores - top)
                top_ref[...] = top
                sum_ref[...] = sum_ref[...] * shrink + jnp.sum(weights, axis=0, keepdims=True)
                acc_ref[...] = acc_ref[...] * shrink + dot(
                    value_ref[group, 0:HD, here], weights.astype(BF)
                )

            context_ref[pl.ds(pl.multiple_of(head * HD, HD), HD), :] = acc_ref[...] / sum_ref[...]


STEP = 1024
STEPS = FF // STEP
CHUNK = 5


def last_kernel(
    moves,
    rate_s,
    tok_ref,
    gain_ref,
    q_ref,
    part_ref,
    pay_ref,
    w_out_hbm,
    w_obs_hbm,
    w_up_hbm,
    w_down_hbm,
    *rest,
):
    blocks = rest[:LON]
    (
        out_ref,
        w_out_ref,
        w_obs_ref,
        w_up_ref,
        w_down_ref,
        key_ref,
        value_ref,
        context_ref,
        largest_ref,
        ahead_ref,
        top_ref,
        sum_ref,
        acc_ref,
        sem,
    ) = rest[LON:]
    copies = [
        pltpu.make_async_copy(w_out_hbm, w_out_ref, sem.at[0]),
        pltpu.make_async_copy(w_obs_hbm, w_obs_ref, sem.at[1]),
    ]
    for s in range(STEPS):
        here = pl.ds(s * STEP, STEP)
        copies.append(pltpu.make_async_copy(w_up_hbm.at[:, here], w_up_ref.at[s], sem.at[2 + 2 * s]))
        copies.append(
            pltpu.make_async_copy(w_down_hbm.at[here, :], w_down_ref.at[s], sem.at[3 + 2 * s])
        )
    for copy in copies:
        copy.start()

    ahead = ahead_of(moves)
    lane = iota((ROWS, 128), 1)
    for b in range(LON):
        here = pl.ds(b * ROWS, ROWS)
        extra = (place_lanes(ahead[b], HD), place_lanes(ahead[b], 0))
        for group in range(KVH):
            odd = group % 2
            pair = blocks[b][0:ROWS, (group // 2) * 128 : (group // 2) * 128 + 128]
            key_ref[group, here, :] = jnp.where((lane < HD) == (odd == 0), pair, extra[odd])
            value_ref[group, :, here] = value_rows(blocks[b], group)
    gap = LON // 2 * ROWS - jnp.abs(iota((ROWS, ROWS), 0) - iota((ROWS, ROWS), 1))
    gap = gap.astype(F32)
    largest_ref[...] = jnp.zeros((1, ROWS), F32)

    @pl.loop(0, KVH)
    def _(group):
        for i in range(4):
            head = group * 4 + i
            total = part_ref[head]
            for first in range(1, LON, CHUNK):
                here = pl.ds(first * ROWS, CHUNK * ROWS)
                scores = dot(key_ref[group, here, :], q_ref[head])
                if first == 1:
                    far = scores[:ROWS] - (rate_s[head] * LOG2E) * gap
                    scores = jnp.concatenate([far, scores[ROWS:]], axis=0)
                total = total + dot(value_ref[group, :, here], jnp.exp2(scores).astype(BF))
            weight_sum = total[HD : HD + 1]
            largest_ref[...] = jnp.maximum(largest_ref[...], weight_sum)
            context_ref[pl.ds(pl.multiple_of(head * HD, HD), HD), :] = total[:HD] * (
                1.0 / weight_sum
            )

    @pl.when(jnp.logical_not(jnp.max(largest_ref[...]) < 2.0**100))
    def _():
        careful(
            ahead, rate_s, q_ref, key_ref, value_ref, ahead_ref, context_ref, top_ref, sum_ref, acc_ref
        )

    pay = jnp.concatenate([pay_ref[:, 0, :], pay_ref[:, 1, :]], axis=0)
    cell = pay[:, D:PAY].astype(F32).T
    cell = jnp.broadcast_to(cell[0:1, :], (ROWS, SLOTS)).astype(I32)
    place = (iota((ROWS, SLOTS), 0) + 1 == cell).astype(F32).astype(BF)
    pooled = dot(place, pay[:, 0:D]).astype(BF)
    context = context_ref[...].T.astype(BF)
    copies[0].wait()
    mixed = tok_ref[...].astype(F32) + dot(context, w_out_ref[...])
    copies[1].wait()
    mixed = (mixed + dot(pooled, w_obs_ref[...])).astype(BF).astype(F32)
    normed = normed_rows(mixed, gain_ref[...])
    for s in range(STEPS):
        copies[2 + 2 * s].wait()
        hidden = (0.5 * twice_gelu(dot(normed, w_up_ref[s]))).astype(BF)
        copies[3 + 2 * s].wait()
        mixed = mixed + dot(hidden, w_down_ref[s])
    out_ref[...] = mixed.astype(BF)


def last_call(moves, head_rate, tokens, gain, q, part, pay, w_out, w_obs_out, w_up, w_down, blocks):
    return pl.pallas_call(
        functools.partial(last_kernel, moves),
        out_shape=jax.ShapeDtypeStruct((ROWS, D), BF),
        in_specs=[SMEM] + [VMEM] * 5 + [ANY] * 4 + [VMEM] * LON,
        out_specs=VMEM,
        scratch_shapes=[
            pltpu.VMEM((D, D), BF),
            pltpu.VMEM((D, D), BF),
            pltpu.VMEM((STEPS, D, STEP), BF),
            pltpu.VMEM((STEPS, STEP, D), BF),
            pltpu.VMEM((KVH, BAND, 128), BF),
            pltpu.VMEM((KVH, VT, BAND), BF),
            pltpu.VMEM((D, ROWS), F32),
            pltpu.VMEM((1, ROWS), F32),
            pltpu.SMEM((LON,), I32),
            pltpu.VMEM((1, ROWS), F32),
            pltpu.VMEM((1, ROWS), F32),
            pltpu.VMEM((HD, ROWS), F32),
            pltpu.SemaphoreType.DMA((2 + 2 * STEPS,)),
        ],
        compiler_params=params(60),
        cost_estimate=cost(24),
        name="other_rows_project_update_mlp",
    )(
        head_rate,
        tokens,
        gain.reshape(1, D),
        q,
        part,
        pay,
        w_out,
        w_obs_out,
        w_up,
        w_down,
        *blocks,
    )


def lon_of(x, z, core):
    return x * 8 + (z % 4) * 2 + core


def send(block, flip_x, step_z, flip_core):
    pairs = [
        (lon_of(x, z, core), lon_of(x ^ flip_x, z + step_z, core ^ flip_core))
        for x in range(2)
        for z in range(4)
        for core in range(2)
    ]
    return lax.ppermute(block, "lon", pairs)


def ahead_of(moves):
    me = lax.axis_index("lon")
    x, z, core = me // 8, (me // 2) % 4, me % 2
    sources = [
        lax.rem(x + fx, 2) * 8 + lax.rem(z + 4 - dz, 4) * 2 + lax.rem(core + fc, 2)
        for fx, dz, fc in moves
    ]
    return [lax.rem(s - me + LON, LON) for s in sources]


def shards(
    tokens,
    attn_gain,
    w_query,
    w_key,
    w_value,
    w_out,
    head_rate,
    obs_values,
    tile_owner,
    tile_cell,
    tile_count,
    w_obs_in,
    w_obs_out,
    mlp_gain,
    w_up,
    w_down,
):
    normed, kv = kv_call(tokens, attn_gain, w_key, w_value)
    up = send(kv, 0, 1, 0)
    down = send(kv, 0, 3, 0)
    across = send(kv, 1, 0, 0)
    far = send(kv, 0, 2, 0)
    sibling = send(kv, 0, 0, 1)
    pay = pool_call(obs_values, tile_owner, tile_cell, tile_count, w_obs_in)
    pay, normed, up, down, across, far, sibling = lax.optimization_barrier(
        (pay, normed, up, down, across, far, sibling)
    )
    late = [send(across, 0, 1, 0), send(across, 0, 3, 0), send(far, 1, 0, 0)]
    near = [across, up, down, far]
    near_twin = [send(b, 0, 0, 1) for b in near]
    pay = lax.all_to_all(pay, ("lat", "lon"), split_axis=0, concat_axis=0, tiled=True)
    q, part = first_call(head_rate, normed, w_query, kv)
    late_twin = [send(b, 0, 0, 1) for b in late]

    near_moves = [(1, 0, 0), (0, 1, 0), (0, 3, 0), (0, 2, 0)]
    late_moves = [(1, 1, 0), (1, 3, 0), (1, 2, 0)]
    moves = [(0, 0, 0)] + near_moves + late_moves + [(0, 0, 1)]
    moves = moves + [(x, z, 1) for x, z, _ in near_moves + late_moves]
    return last_call(
        moves,
        head_rate,
        tokens,
        mlp_gain,
        q,
        part,
        pay,
        w_out,
        w_obs_out,
        w_up,
        w_down,
        [kv] + near + late + [sibling] + near_twin + late_twin,
    )


def solution(mesh):
    shard = P(("lat", "lon"))
    rows = P(("lat", "lon"), None)
    return jax.shard_map(
        shards,
        mesh=mesh,
        in_specs=(rows,)
        + (P(),) * 6
        + (P(("lat", "lon"), None, None), rows, shard, shard)
        + (P(),) * 5,
        out_specs=rows,
        check_vma=False,
    )
```

```python
import functools
import math

import jax
import jax.numpy as jnp
from jax import lax
from jax.experimental import pallas as pl
from jax.experimental.pallas import tpu as pltpu
from jax.sharding import PartitionSpec as P

BF = jnp.bfloat16
F32 = jnp.float32
I32 = jnp.int32

D = 1024
HEADS = 16
HD = 64
KVH = 4
FF = 4096
ROWS = 256
TILES = 128
TROWS = 128
F_OBS = 32
LON = 16
BAND = ROWS * LON
SLOTS = 256
PAY = D + 128
LOG2E = 1.4426950408889634
VT = HD + 16
MIB = 2**20
VMEM = pl.BlockSpec(memory_space=pltpu.VMEM)
SMEM = pl.BlockSpec(memory_space=pltpu.SMEM)
ANY = pl.BlockSpec(memory_space=pl.ANY)


def iota(shape, dim):
    return lax.broadcasted_iota(I32, shape, dim)


def params(mib):
    return pltpu.CompilerParams(vmem_limit_bytes=mib * MIB)


def cost(micros):
    return pl.CostEstimate(
        flops=int(micros * 1.0e9), bytes_accessed=int(micros * 1.0e6), transcendentals=0
    )


def dot(a, b):
    return jnp.dot(a, b, preferred_element_type=F32)


def normed_rows(rows, gain):
    mean_square = jnp.mean(rows * rows, axis=-1, keepdims=True)
    return (rows * lax.rsqrt(mean_square + 1e-05) * gain).astype(BF)


def twice_gelu(x):
    k0 = math.sqrt(2.0 / math.pi)
    k1 = k0 * 0.044715
    inner = x * (x * x * k1 + k0)
    return jnp.tanh(inner) * x + x


def kv_kernel(tok_ref, gain_ref, wk_ref, wv_ref, normed_ref, kv_ref):
    normed = normed_rows(tok_ref[...].astype(F32), gain_ref[...])
    normed_ref[...] = normed
    kv_ref[0:ROWS, :] = dot(normed, wk_ref[...]).astype(BF)
    kv_ref[ROWS : 2 * ROWS, :] = dot(normed, wv_ref[...]).T.astype(BF)


def kv_call(tokens, gain, w_key, w_value):
    return pl.pallas_call(
        kv_kernel,
        out_shape=(
            jax.ShapeDtypeStruct((ROWS, D), BF),
            jax.ShapeDtypeStruct((2 * ROWS, KVH * HD), BF),
        ),
        in_specs=[VMEM] * 4,
        out_specs=(VMEM, VMEM),
        compiler_params=params(60),
        cost_estimate=cost(3),
        name="norm_keys_values",
    )(tokens, gain.reshape(1, D), w_key, w_value)


BLOCK = 512
HALF = BLOCK // 2
COLS = 512


def pool_kernel(
    cnt_s, obs_ref, cnt_ref, own_ref, cell_ref, w_ref, pay_ref, live_ref, acc_ref, act_ref, member_ref
):
    square = (TILES, TILES)
    source = iota(square, 1) // F_OBS
    row = iota(square, 0)

    def put(step, first):
        for u in range(2):
            four = step * 2 + u
            rows = obs_ref[pl.ds(pl.multiple_of(four * TILES, TILES), TILES), :].T
            for k in range(4):
                count = cnt_s[four * 4 + k]
                live_ref[pl.ds(pl.multiple_of(first, 32), TROWS), :] = jnp.where(
                    (source == k) & (row < count), rows, jnp.zeros_like(rows)
                )
                first = first + ((count + 31) // 32) * 32
        return first

    total = lax.fori_loop(0, TILES // 8, put, jnp.int32(0))
    for i in range(0, 2 * BLOCK, 128):
        live_ref[pl.ds(pl.multiple_of(total + i, 32), 128), :] = jnp.zeros(square, BF)

    weights = jnp.concatenate([w_ref[...]] * 4, axis=0)
    cnt = jnp.broadcast_to(cnt_ref[...].astype(F32), square).T
    groups = jnp.floor((cnt + 31.0) * (1.0 / 32.0))
    earlier = (iota(square, 1) < iota(square, 0)).astype(F32)
    start = dot(earlier.astype(BF), groups.astype(BF)) * 16.0
    start = jnp.concatenate([start] * (HALF // 128), axis=1)
    length = jnp.concatenate([groups * 16.0] * (HALF // 128), axis=1)

    acc_ref[...] = jnp.zeros_like(acc_ref)
    act_ref[...] = jnp.zeros_like(act_ref)
    member_ref[...] = jnp.zeros_like(member_ref)

    def one_block(block, now):
        old = 1 - now
        rows = live_ref[pl.ds(pl.multiple_of(block * BLOCK, BLOCK), BLOCK), :]
        place = (iota((TILES, HALF), 1) + block * HALF).astype(F32) - start
        member_ref[now] = ((place >= 0) & (place < length)).astype(F32).astype(BF)
        for c in range(0, D, COLS):
            here = slice(c, c + COLS)
            x = dot(rows, weights[:, here])
            acc_ref[:, here] += dot(member_ref[old], act_ref[old, :, here])
            act = twice_gelu(x.astype(BF))
            act_ref[now, :, here] = jnp.concatenate(
                [act[i : i + 16] + act[i + 16 : i + 32] for i in range(0, BLOCK, 32)], axis=0
            )

    @pl.loop(0, (total + 2 * BLOCK - 1) // (2 * BLOCK))
    def _(pair):
        one_block(2 * pair, 0)
        one_block(2 * pair + 1, 1)

    pooled = (acc_ref[...] + dot(member_ref[1], act_ref[1])) * (0.5 / cnt[:, 0:1])
    own_t = jnp.broadcast_to(own_ref[...].astype(F32), square)
    rank = jnp.sum(
        jnp.where((own_t.T == own_t) & (iota(square, 0) < iota(square, 1)), 1.0, 0.0),
        axis=0,
        keepdims=True,
    )
    slot = (2.0 * own_t[0:1, :] + rank).astype(I32)
    cell = (jnp.broadcast_to(cell_ref[...].astype(F32), square).T + 1.0).astype(BF)
    for k in range(2):
        place = (2 * iota(square, 0) + k == slot).astype(F32).astype(BF)
        pay_ref[:, k, 0:D] = dot(place, pooled.astype(BF)).astype(BF)
        pay_ref[:, k, D:PAY] = dot(place, cell).astype(BF)


def pool_call(obs_values, tile_owner, tile_cell, tile_count, w_obs_in):
    return pl.pallas_call(
        pool_kernel,
        out_shape=jax.ShapeDtypeStruct((SLOTS // 2, 2, PAY), BF),
        in_specs=[SMEM] + [VMEM] * 5,
        out_specs=VMEM,
        scratch_shapes=[
            pltpu.VMEM((TILES * TROWS + 2 * BLOCK, 128), BF),
            pltpu.VMEM((TILES, D), F32),
            pltpu.VMEM((2, HALF, D), BF),
            pltpu.VMEM((2, TILES, HALF), BF),
        ],
        compiler_params=params(60),
        cost_estimate=cost(15),
        name="pool_tiles",
    )(
        tile_count,
        jnp.transpose(obs_values, (0, 2, 1)).reshape(TILES * F_OBS, TROWS),
        tile_count.reshape(1, TILES),
        tile_owner.reshape(1, TILES),
        tile_cell.reshape(1, TILES),
        w_obs_in,
    )


def three(x):
    hi = x.astype(BF)
    rest = x - hi.astype(F32)
    mid = rest.astype(BF)
    lo = (rest - mid.astype(F32)).astype(BF)
    return [hi.astype(F32), mid.astype(F32), lo.astype(F32)]


def stacked(rows, count):
    place = iota((count, ROWS), 0)
    out = jnp.zeros((count, ROWS), F32)
    for i, row in enumerate(rows):
        out = jnp.where(place == i, jnp.broadcast_to(row, out.shape), out)
    return out


def value_rows(kv_ref, group):
    first = ROWS + group * HD
    return jnp.concatenate([kv_ref[first : first + HD, :], jnp.ones((VT - HD, ROWS), BF)], axis=0)


def place_lanes(first):
    lane = iota((ROWS, 128), 1) - first
    row = iota((ROWS, 128), 0)

    def lanes(low, value):
        return jnp.where((lane >= low) & (lane < low + 3), value, 0)

    parts = (lanes(0, -row) + lanes(6, 1), lanes(0, row) + lanes(9, 1), lanes(12, 1), lanes(3, -ROWS))
    return [p.astype(F32).astype(BF) for p in parts]


def beside_keys(parts, ahead):
    blocks = jnp.where(ahead < 8, ahead, LON - ahead).astype(F32)
    blocks = jnp.full((ROWS, 128), blocks, F32).astype(BF)
    return jnp.where(ahead < 8, parts[0], parts[1]) + parts[3] * blocks


def lay_out(blocks, aheads, half_way, key_ref, value_ref):
    lane = iota((ROWS, 128), 1)
    parts = (place_lanes(HD), place_lanes(0))
    for b, block in enumerate(blocks):
        here = pl.ds(b * ROWS, ROWS)
        extra = [p[2] if b == half_way else beside_keys(p, aheads[b]) for p in parts]
        for group in range(KVH):
            odd = group % 2
            pair = block[0:ROWS, (group // 2) * 128 : (group // 2) * 128 + 128]
            key_ref[group, here, :] = jnp.where((lane < HD) == (odd == 0), pair, extra[odd])
            value_ref[group, :, here] = value_rows(block, group)


def attend(total, group, head, chunks, gap, rate_s, q_ref, key_ref, value_ref):
    first = 0
    for size in chunks:
        here = pl.ds(first * ROWS, size * ROWS)
        scores = dot(key_ref[group, here, :], q_ref[head])
        if gap is not None and first == 0:
            far = scores[:ROWS] - (rate_s[head] * LOG2E) * gap
            scores = jnp.concatenate([far, scores[ROWS:]], axis=0)
        total = total + dot(value_ref[group, :, here], jnp.exp2(scores).astype(BF))
        first = first + size
    return total


NEAR = (5, 4)


def first_kernel(moves, rate_s, normed_ref, wq_ref, kv_ref, *rest):
    blocks = rest[: len(moves)]
    q_ref, out_ref, dist_ref, key_ref, value_ref = rest[len(moves) :]
    q = (dot(normed_ref[...], wq_ref[...]) * (0.125 * LOG2E)).T
    dist_ref[...] = jnp.abs(iota((ROWS, ROWS), 0) - iota((ROWS, ROWS), 1)).astype(F32)
    lane = iota((ROWS, 128), 1)
    at = iota((1, ROWS), 1).astype(F32)
    for group in range(KVH):
        even = group % 2 == 0
        pair = kv_ref[0:ROWS, (group // 2) * 128 : (group // 2) * 128 + 128]
        keys = jnp.where((lane < HD) == even, pair, jnp.zeros_like(pair))
        values = value_rows(kv_ref, group)
        for head in range(4 * group, 4 * group + 4):
            rate = rate_s[head] * LOG2E
            own = q[head * HD : head * HD + HD, :].astype(BF)
            blank = jnp.zeros((HD, ROWS), BF)
            scores = dot(keys, jnp.concatenate([own, blank] if even else [blank, own], axis=0))
            scores = scores - rate * dist_ref[...]
            top = jnp.max(scores, axis=0, keepdims=True)
            out_ref[head] = dot(values, jnp.exp2(scores - top).astype(BF))
            rates = three(jnp.full((1, ROWS), rate, F32))
            extra = stacked(
                rates + rates + three(rate * at - top) + three(-rate * at - top) + three(-top), 16
            ).astype(BF)
            extra = jnp.concatenate([extra, jnp.zeros((HD - 16, ROWS), BF)], axis=0)
            q_ref[head] = jnp.concatenate([own, extra] if even else [extra, own], axis=0)

    lay_out(blocks, ahead_of(moves), 0, key_ref, value_ref)
    gap = LON // 2 * ROWS - dist_ref[...]

    @pl.loop(0, KVH)
    def _(group):
        for i in range(4):
            head = group * 4 + i
            out_ref[head] = attend(
                out_ref[head], group, head, NEAR, gap, rate_s, q_ref, key_ref, value_ref
            )


def first_call(moves, head_rate, normed, w_query, kv, blocks):
    count = len(blocks)
    return pl.pallas_call(
        functools.partial(first_kernel, moves),
        out_shape=(
            jax.ShapeDtypeStruct((HEADS, 128, ROWS), BF),
            jax.ShapeDtypeStruct((HEADS, VT, ROWS), F32),
        ),
        in_specs=[SMEM] + [VMEM] * (3 + count),
        out_specs=(VMEM, VMEM),
        scratch_shapes=[
            pltpu.VMEM((ROWS, ROWS), F32),
            pltpu.VMEM((KVH, count * ROWS, 128), BF),
            pltpu.VMEM((KVH, VT, count * ROWS), BF),
        ],
        compiler_params=params(60),
        cost_estimate=cost(18),
        name="queries_near_rows",
    )(head_rate, normed, w_query, kv, *blocks)


def careful(
    blocks, aheads, rate_s, q_ref, kvs_ref, ahead_ref, context_ref, top_ref, sum_ref, acc_ref, sem
):
    for b in range(LON):
        ahead_ref[b] = aheads[b]
        copy = pltpu.make_async_copy(blocks[b], kvs_ref.at[b], sem)
        copy.start()
        copy.wait()
    lane = iota((ROWS, 128), 1)
    for group in range(KVH):

        @pl.loop(0, 4)
        def _(i):
            head = group * 4 + i
            top_ref[...] = jnp.full((1, ROWS), -jnp.inf, F32)
            sum_ref[...] = jnp.zeros((1, ROWS), F32)
            acc_ref[...] = jnp.zeros((HD, ROWS), F32)

            @pl.loop(0, LON)
            def _(b):
                keys = kvs_ref[b, 0:ROWS, (group // 2) * 128 : (group // 2) * 128 + 128]
                keys = jnp.where((lane < HD) == (group % 2 == 0), keys, jnp.zeros_like(keys))
                gap = jnp.abs(ahead_ref[b] * ROWS + iota((ROWS, ROWS), 0) - iota((ROWS, ROWS), 1))
                gap = jnp.minimum(gap, BAND - gap).astype(F32)
                scores = dot(keys, q_ref[head]) - (rate_s[head] * LOG2E) * gap
                top = jnp.maximum(top_ref[...], jnp.max(scores, axis=0, keepdims=True))
                shrink = jnp.exp2(top_ref[...] - top)
                weights = jnp.exp2(scores - top)
                top_ref[...] = top
                sum_ref[...] = sum_ref[...] * shrink + jnp.sum(weights, axis=0, keepdims=True)
                acc_ref[...] = acc_ref[...] * shrink + dot(
                    kvs_ref[b, ROWS + group * HD : ROWS + group * HD + HD, :], weights.astype(BF)
                )

            context_ref[pl.ds(pl.multiple_of(head * HD, HD), HD), :] = acc_ref[...] / sum_ref[...]


STEP = 2048
STEPS = FF // STEP
LATE = (3, 3)


def last_kernel(
    moves,
    rate_s,
    tok_ref,
    gain_ref,
    q_ref,
    part_ref,
    pay_ref,
    w_out_hbm,
    w_obs_hbm,
    w_up_hbm,
    w_down_hbm,
    *rest,
):
    blocks = rest[:LON]
    count = sum(LATE)
    late = rest[LON : LON + count]
    (
        out_ref,
        w_out_ref,
        w_obs_ref,
        w_up_ref,
        w_down_ref,
        key_ref,
        value_ref,
        context_ref,
        largest_ref,
        ahead_ref,
        top_ref,
        sum_ref,
        acc_ref,
        kvs_ref,
        sem,
        spare,
    ) = rest[LON + count :]
    copies = [
        pltpu.make_async_copy(w_out_hbm, w_out_ref, sem.at[0]),
        pltpu.make_async_copy(w_obs_hbm, w_obs_ref, sem.at[1]),
    ]
    for s in range(STEPS):
        here = pl.ds(s * STEP, STEP)
        copies.append(pltpu.make_async_copy(w_up_hbm.at[:, here], w_up_ref.at[s], sem.at[2 + 2 * s]))
        copies.append(
            pltpu.make_async_copy(w_down_hbm.at[here, :], w_down_ref.at[s], sem.at[3 + 2 * s])
        )
    for copy in copies:
        copy.start()

    aheads = ahead_of(moves)
    lay_out(late, aheads[LON - count :], None, key_ref, value_ref)
    largest_ref[...] = jnp.zeros((1, ROWS), F32)

    @pl.loop(0, KVH)
    def _(group):
        for i in range(4):
            head = group * 4 + i
            total = attend(
                part_ref[head], group, head, LATE, None, rate_s, q_ref, key_ref, value_ref
            )
            weight_sum = total[HD : HD + 1]
            largest_ref[...] = jnp.maximum(largest_ref[...], weight_sum)
            context_ref[pl.ds(pl.multiple_of(head * HD, HD), HD), :] = total[:HD] * (
                1.0 / weight_sum
            )

    @pl.when(jnp.logical_not(jnp.max(largest_ref[...]) < 2.0**100))
    def _():
        careful(
            blocks,
            aheads,
            rate_s,
            q_ref,
            kvs_ref,
            ahead_ref,
            context_ref,
            top_ref,
            sum_ref,
            acc_ref,
            spare,
        )

    pay = jnp.concatenate([pay_ref[:, 0, :], pay_ref[:, 1, :]], axis=0)
    cell = pay[:, D:PAY].astype(F32).T
    cell = jnp.broadcast_to(cell[0:1, :], (ROWS, SLOTS)).astype(I32)
    place = (iota((ROWS, SLOTS), 0) + 1 == cell).astype(F32).astype(BF)
    pooled = dot(place, pay[:, 0:D]).astype(BF)
    context = context_ref[...].T.astype(BF)
    copies[0].wait()
    mixed = tok_ref[...].astype(F32) + dot(context, w_out_ref[...])
    copies[1].wait()
    mixed = (mixed + dot(pooled, w_obs_ref[...])).astype(BF).astype(F32)
    normed = normed_rows(mixed, gain_ref[...])
    for copy in copies[2:]:
        copy.wait()
    for s in range(STEPS):
        hidden = (0.5 * twice_gelu(dot(normed, w_up_ref[s]))).astype(BF)
        mixed = mixed + dot(hidden, w_down_ref[s])
    out_ref[...] = mixed.astype(BF)


def last_call(moves, head_rate, tokens, gain, q, part, pay, w_out, w_obs_out, w_up, w_down, blocks):
    return pl.pallas_call(
        functools.partial(last_kernel, moves),
        out_shape=jax.ShapeDtypeStruct((ROWS, D), BF),
        in_specs=[SMEM] + [VMEM] * 5 + [ANY] * (4 + LON) + [VMEM] * sum(LATE),
        out_specs=VMEM,
        scratch_shapes=[
            pltpu.VMEM((D, D), BF),
            pltpu.VMEM((D, D), BF),
            pltpu.VMEM((STEPS, D, STEP), BF),
            pltpu.VMEM((STEPS, STEP, D), BF),
            pltpu.VMEM((KVH, sum(LATE) * ROWS, 128), BF),
            pltpu.VMEM((KVH, VT, sum(LATE) * ROWS), BF),
            pltpu.VMEM((D, ROWS), F32),
            pltpu.VMEM((1, ROWS), F32),
            pltpu.SMEM((LON,), I32),
            pltpu.VMEM((1, ROWS), F32),
            pltpu.VMEM((1, ROWS), F32),
            pltpu.VMEM((HD, ROWS), F32),
            pltpu.VMEM((LON, 2 * ROWS, KVH * HD), BF),
            pltpu.SemaphoreType.DMA((2 + 2 * STEPS,)),
            pltpu.SemaphoreType.DMA,
        ],
        compiler_params=params(60),
        cost_estimate=cost(17),
        name="late_rows_project_update_mlp",
    )(
        head_rate,
        tokens,
        gain.reshape(1, D),
        q,
        part,
        pay,
        w_out,
        w_obs_out,
        w_up,
        w_down,
        *blocks,
        *blocks[LON - sum(LATE) :],
    )


def lon_of(x, z, core):
    return x * 8 + (z % 4) * 2 + core


def send(block, flip_x, step_z, flip_core):
    pairs = [
        (lon_of(x, z, core), lon_of(x ^ flip_x, z + step_z, core ^ flip_core))
        for x in range(2)
        for z in range(4)
        for core in range(2)
    ]
    return lax.ppermute(block, "lon", pairs)


def ahead_of(moves):
    me = lax.axis_index("lon")
    x, z, core = me // 8, (me // 2) % 4, me % 2
    sources = [
        lax.rem(x + fx, 2) * 8 + lax.rem(z + 4 - dz, 4) * 2 + lax.rem(core + fc, 2)
        for fx, dz, fc in moves
    ]
    return [lax.rem(s - me + LON, LON) for s in sources]


def shards(
    tokens,
    attn_gain,
    w_query,
    w_key,
    w_value,
    w_out,
    head_rate,
    obs_values,
    tile_owner,
    tile_cell,
    tile_count,
    w_obs_in,
    w_obs_out,
    mlp_gain,
    w_up,
    w_down,
):
    normed, kv = kv_call(tokens, attn_gain, w_key, w_value)
    up = send(kv, 0, 1, 0)
    down = send(kv, 0, 3, 0)
    across = send(kv, 1, 0, 0)
    far = send(kv, 0, 2, 0)
    sibling = send(kv, 0, 0, 1)
    pay = pool_call(obs_values, tile_owner, tile_cell, tile_count, w_obs_in)
    pay, normed, up, down, across, far, sibling = lax.optimization_barrier(
        (pay, normed, up, down, across, far, sibling)
    )
    late = [send(across, 0, 1, 0), send(across, 0, 3, 0), send(far, 1, 0, 0)]
    near = [across, up, down, far]
    near_twin = [send(b, 0, 0, 1) for b in near]
    pay = lax.all_to_all(pay, ("lat", "lon"), split_axis=0, concat_axis=0, tiled=True)
    late_twin = [send(b, 0, 0, 1) for b in late]

    near_moves = [(1, 0, 0), (0, 1, 0), (0, 3, 0), (0, 2, 0)]
    late_moves = [(1, 1, 0), (1, 3, 0), (1, 2, 0)]
    near_moves = near_moves + [(0, 0, 1)] + [(x, z, 1) for x, z, _ in near_moves]
    late_moves = late_moves + [(x, z, 1) for x, z, _ in late_moves]
    near = near + [sibling] + near_twin
    q, part = first_call(near_moves, head_rate, normed, w_query, kv, near)
    return last_call(
        [(0, 0, 0)] + near_moves + late_moves,
        head_rate,
        tokens,
        mlp_gain,
        q,
        part,
        pay,
        w_out,
        w_obs_out,
        w_up,
        w_down,
        [kv] + near + late + late_twin,
    )


def solution(mesh):
    shard = P(("lat", "lon"))
    rows = P(("lat", "lon"), None)
    return jax.shard_map(
        shards,
        mesh=mesh,
        in_specs=(rows,)
        + (P(),) * 6
        + (P(("lat", "lon"), None, None), rows, shard, shard)
        + (P(),) * 5,
        out_specs=rows,
        check_vma=False,
    )
```

```python
import functools
import math

import jax
import jax.numpy as jnp
from jax import lax
from jax.experimental import pallas as pl
from jax.experimental.pallas import tpu as pltpu
from jax.sharding import PartitionSpec as P

BF = jnp.bfloat16
F32 = jnp.float32
I32 = jnp.int32

D = 1024
HEADS = 16
HD = 64
KVH = 4
FF = 4096
ROWS = 256
TILES = 128
TROWS = 128
F_OBS = 32
LON = 16
BAND = ROWS * LON
SLOTS = 256
PAY = D + 128
LOG2E = 1.4426950408889634
VT = HD + 16
MIB = 2**20
VMEM = pl.BlockSpec(memory_space=pltpu.VMEM)
SMEM = pl.BlockSpec(memory_space=pltpu.SMEM)
ANY = pl.BlockSpec(memory_space=pl.ANY)


def iota(shape, dim):
    return lax.broadcasted_iota(I32, shape, dim)


def params(mib):
    return pltpu.CompilerParams(vmem_limit_bytes=mib * MIB)


def cost(micros):
    return pl.CostEstimate(
        flops=int(micros * 1.0e9), bytes_accessed=int(micros * 1.0e6), transcendentals=0
    )


def dot(a, b):
    return jnp.dot(a, b, preferred_element_type=F32)


def normed_rows(rows, gain):
    mean_square = jnp.mean(rows * rows, axis=-1, keepdims=True)
    return (rows * lax.rsqrt(mean_square + 1e-05) * gain).astype(BF)


def twice_gelu(x):
    k0 = math.sqrt(2.0 / math.pi)
    k1 = k0 * 0.044715
    inner = x * (x * x * k1 + k0)
    return jnp.tanh(inner) * x + x


def kv_kernel(tok_ref, gain_ref, wk_ref, wv_ref, normed_ref, kv_ref):
    normed = normed_rows(tok_ref[...].astype(F32), gain_ref[...])
    normed_ref[...] = normed
    kv_ref[0:ROWS, :] = dot(normed, wk_ref[...]).astype(BF)
    kv_ref[ROWS : 2 * ROWS, :] = dot(normed, wv_ref[...]).T.astype(BF)


def kv_call(tokens, gain, w_key, w_value):
    return pl.pallas_call(
        kv_kernel,
        out_shape=(
            jax.ShapeDtypeStruct((ROWS, D), BF),
            jax.ShapeDtypeStruct((2 * ROWS, KVH * HD), BF),
        ),
        in_specs=[VMEM] * 4,
        out_specs=(VMEM, VMEM),
        compiler_params=params(60),
        cost_estimate=cost(3),
        name="norm_keys_values",
    )(tokens, gain.reshape(1, D), w_key, w_value)


BLOCK = 512
HALF = BLOCK // 2
COLS = 512


def pool_kernel(
    cnt_s, obs_ref, cnt_ref, own_ref, cell_ref, w_ref, pay_ref, live_ref, acc_ref, act_ref, member_ref
):
    square = (TILES, TILES)
    lanes = [(iota(square, 1) // F_OBS == k).astype(F32).astype(BF) for k in range(4)]
    column = iota(square, 1)

    def put(step, first):
        for u in range(4):
            four = step * 4 + u
            counts = [cnt_s[four * 4 + k] for k in range(4)]
            limit = jnp.concatenate([jnp.full((F_OBS, TROWS), c, I32) for c in counts], axis=0)
            rows = obs_ref[pl.ds(pl.multiple_of(four * TILES, TILES), TILES), :]
            rows = jnp.where(column < limit, rows, jnp.zeros_like(rows)).T
            for k, count in enumerate(counts):
                live_ref[pl.ds(pl.multiple_of(first, 32), TROWS), :] = rows * lanes[k]
                first = first + ((count + 31) // 32) * 32
        return first

    total = lax.fori_loop(0, TILES // 16, put, jnp.int32(0))
    for i in range(0, 2 * BLOCK, 128):
        live_ref[pl.ds(pl.multiple_of(total + i, 32), 128), :] = jnp.zeros(square, BF)

    weights = jnp.concatenate([w_ref[...]] * 4, axis=0)
    cnt = jnp.broadcast_to(cnt_ref[...].astype(F32), square).T
    groups = jnp.floor((cnt + 31.0) * (1.0 / 32.0))
    earlier = (iota(square, 1) < iota(square, 0)).astype(F32)
    start = dot(earlier.astype(BF), groups.astype(BF)) * 16.0
    start = jnp.concatenate([start] * (HALF // 128), axis=1)
    length = jnp.concatenate([groups * 16.0] * (HALF // 128), axis=1)

    acc_ref[...] = jnp.zeros_like(acc_ref)
    act_ref[...] = jnp.zeros_like(act_ref)
    member_ref[...] = jnp.zeros_like(member_ref)

    def one_block(block, now):
        old = 1 - now
        rows = live_ref[pl.ds(pl.multiple_of(block * BLOCK, BLOCK), BLOCK), :]
        place = (iota((TILES, HALF), 1) + block * HALF).astype(F32) - start
        member_ref[now] = ((place >= 0) & (place < length)).astype(F32).astype(BF)
        for c in range(0, D, COLS):
            here = slice(c, c + COLS)
            x = dot(rows, weights[:, here])
            acc_ref[:, here] += dot(member_ref[old], act_ref[old, :, here])
            act = twice_gelu(x.astype(BF))
            act_ref[now, :, here] = jnp.concatenate(
                [act[i : i + 16] + act[i + 16 : i + 32] for i in range(0, BLOCK, 32)], axis=0
            )

    @pl.loop(0, (total + 2 * BLOCK - 1) // (2 * BLOCK))
    def _(pair):
        one_block(2 * pair, 0)
        one_block(2 * pair + 1, 1)

    pooled = (acc_ref[...] + dot(member_ref[1], act_ref[1])) * (0.5 / cnt[:, 0:1])
    own_t = jnp.broadcast_to(own_ref[...].astype(F32), square)
    rank = jnp.sum(
        jnp.where((own_t.T == own_t) & (iota(square, 0) < iota(square, 1)), 1.0, 0.0),
        axis=0,
        keepdims=True,
    )
    slot = (2.0 * own_t[0:1, :] + rank).astype(I32)
    cell = (jnp.broadcast_to(cell_ref[...].astype(F32), square).T + 1.0).astype(BF)
    for k in range(2):
        place = (2 * iota(square, 0) + k == slot).astype(F32).astype(BF)
        pay_ref[:, k, 0:D] = dot(place, pooled.astype(BF)).astype(BF)
        pay_ref[:, k, D:PAY] = dot(place, cell).astype(BF)


def pool_call(obs_values, tile_owner, tile_cell, tile_count, w_obs_in):
    return pl.pallas_call(
        pool_kernel,
        out_shape=jax.ShapeDtypeStruct((SLOTS // 2, 2, PAY), BF),
        in_specs=[SMEM] + [VMEM] * 5,
        out_specs=VMEM,
        scratch_shapes=[
            pltpu.VMEM((TILES * TROWS + 2 * BLOCK, 128), BF),
            pltpu.VMEM((TILES, D), F32),
            pltpu.VMEM((2, HALF, D), BF),
            pltpu.VMEM((2, TILES, HALF), BF),
        ],
        compiler_params=params(60),
        cost_estimate=cost(15),
        name="pool_tiles",
    )(
        tile_count,
        jnp.transpose(obs_values, (0, 2, 1)).reshape(TILES * F_OBS, TROWS),
        tile_count.reshape(1, TILES),
        tile_owner.reshape(1, TILES),
        tile_cell.reshape(1, TILES),
        w_obs_in,
    )


def three(x):
    hi = x.astype(BF)
    rest = x - hi.astype(F32)
    mid = rest.astype(BF)
    lo = (rest - mid.astype(F32)).astype(BF)
    return [hi.astype(F32), mid.astype(F32), lo.astype(F32)]


def stacked(rows, count):
    place = iota((count, ROWS), 0)
    out = jnp.zeros((count, ROWS), F32)
    for i, row in enumerate(rows):
        out = jnp.where(place == i, jnp.broadcast_to(row, out.shape), out)
    return out


def value_rows(kv_ref, group):
    first = ROWS + group * HD
    return jnp.concatenate([kv_ref[first : first + HD, :], jnp.ones((VT - HD, ROWS), BF)], axis=0)


def place_lanes(first):
    lane = iota((ROWS, 128), 1) - first
    row = iota((ROWS, 128), 0)

    def lanes(low, value):
        return jnp.where((lane >= low) & (lane < low + 3), value, 0)

    parts = (lanes(0, -row) + lanes(6, 1), lanes(0, row) + lanes(9, 1), lanes(12, 1), lanes(3, -ROWS))
    return [p.astype(F32).astype(BF) for p in parts]


def beside_keys(parts, ahead):
    blocks = jnp.where(ahead < 8, ahead, LON - ahead).astype(F32)
    blocks = jnp.full((ROWS, 128), blocks, F32).astype(BF)
    return jnp.where(ahead < 8, parts[0], parts[1]) + parts[3] * blocks


def lay_out(blocks, aheads, half_way, key_ref, value_ref):
    lane = iota((ROWS, 128), 1)
    parts = (place_lanes(HD), place_lanes(0))
    for b, block in enumerate(blocks):
        here = pl.ds(b * ROWS, ROWS)
        extra = [p[2] if b == half_way else beside_keys(p, aheads[b]) for p in parts]
        for group in range(KVH):
            odd = group % 2
            pair = block[0:ROWS, (group // 2) * 128 : (group // 2) * 128 + 128]
            key_ref[group, here, :] = jnp.where((lane < HD) == (odd == 0), pair, extra[odd])
            value_ref[group, :, here] = value_rows(block, group)


def attend(total, group, head, chunks, gap, rate_s, q_ref, key_ref, value_ref):
    first = 0
    for size in chunks:
        here = pl.ds(first * ROWS, size * ROWS)
        scores = dot(key_ref[group, here, :], q_ref[head])
        if gap is not None and first == 0:
            far = scores[:ROWS] - (rate_s[head] * LOG2E) * gap
            scores = jnp.concatenate([far, scores[ROWS:]], axis=0)
        total = total + dot(value_ref[group, :, here], jnp.exp2(scores).astype(BF))
        first = first + size
    return total


NEAR = (5, 4)


def first_kernel(moves, rate_s, normed_ref, wq_ref, kv_ref, *rest):
    blocks = rest[: len(moves)]
    q_ref, out_ref, dist_ref, key_ref, value_ref = rest[len(moves) :]
    q = (dot(normed_ref[...], wq_ref[...]) * (0.125 * LOG2E)).T
    dist_ref[...] = jnp.abs(iota((ROWS, ROWS), 0) - iota((ROWS, ROWS), 1)).astype(F32)
    lane = iota((ROWS, 128), 1)
    at = iota((1, ROWS), 1).astype(F32)
    for group in range(KVH):
        even = group % 2 == 0
        pair = kv_ref[0:ROWS, (group // 2) * 128 : (group // 2) * 128 + 128]
        keys = jnp.where((lane < HD) == even, pair, jnp.zeros_like(pair))
        values = value_rows(kv_ref, group)
        for head in range(4 * group, 4 * group + 4):
            rate = rate_s[head] * LOG2E
            own = q[head * HD : head * HD + HD, :].astype(BF)
            blank = jnp.zeros((HD, ROWS), BF)
            scores = dot(keys, jnp.concatenate([own, blank] if even else [blank, own], axis=0))
            scores = scores - rate * dist_ref[...]
            top = jnp.max(scores, axis=0, keepdims=True)
            out_ref[head] = dot(values, jnp.exp2(scores - top).astype(BF))
            rates = three(jnp.full((1, ROWS), rate, F32))
            extra = stacked(
                rates + rates + three(rate * at - top) + three(-rate * at - top) + three(-top), 16
            ).astype(BF)
            extra = jnp.concatenate([extra, jnp.zeros((HD - 16, ROWS), BF)], axis=0)
            q_ref[head] = jnp.concatenate([own, extra] if even else [extra, own], axis=0)

    lay_out(blocks, ahead_of(moves), 0, key_ref, value_ref)
    gap = LON // 2 * ROWS - dist_ref[...]

    @pl.loop(0, KVH)
    def _(group):
        for i in range(4):
            head = group * 4 + i
            out_ref[head] = attend(
                out_ref[head], group, head, NEAR, gap, rate_s, q_ref, key_ref, value_ref
            )


def first_call(moves, head_rate, normed, w_query, kv, blocks):
    count = len(blocks)
    return pl.pallas_call(
        functools.partial(first_kernel, moves),
        out_shape=(
            jax.ShapeDtypeStruct((HEADS, 128, ROWS), BF),
            jax.ShapeDtypeStruct((HEADS, VT, ROWS), F32),
        ),
        in_specs=[SMEM] + [VMEM] * (3 + count),
        out_specs=(VMEM, VMEM),
        scratch_shapes=[
            pltpu.VMEM((ROWS, ROWS), F32),
            pltpu.VMEM((KVH, count * ROWS, 128), BF),
            pltpu.VMEM((KVH, VT, count * ROWS), BF),
        ],
        compiler_params=params(60),
        cost_estimate=cost(18),
        name="queries_near_rows",
    )(head_rate, normed, w_query, kv, *blocks)


def careful(
    blocks, aheads, rate_s, q_ref, kvs_ref, ahead_ref, context_ref, top_ref, sum_ref, acc_ref, sem
):
    for b in range(LON):
        ahead_ref[b] = aheads[b]
        copy = pltpu.make_async_copy(blocks[b], kvs_ref.at[b], sem)
        copy.start()
        copy.wait()
    lane = iota((ROWS, 128), 1)
    for group in range(KVH):

        @pl.loop(0, 4)
        def _(i):
            head = group * 4 + i
            top_ref[...] = jnp.full((1, ROWS), -jnp.inf, F32)
            sum_ref[...] = jnp.zeros((1, ROWS), F32)
            acc_ref[...] = jnp.zeros((HD, ROWS), F32)

            @pl.loop(0, LON)
            def _(b):
                keys = kvs_ref[b, 0:ROWS, (group // 2) * 128 : (group // 2) * 128 + 128]
                keys = jnp.where((lane < HD) == (group % 2 == 0), keys, jnp.zeros_like(keys))
                gap = jnp.abs(ahead_ref[b] * ROWS + iota((ROWS, ROWS), 0) - iota((ROWS, ROWS), 1))
                gap = jnp.minimum(gap, BAND - gap).astype(F32)
                scores = dot(keys, q_ref[head]) - (rate_s[head] * LOG2E) * gap
                top = jnp.maximum(top_ref[...], jnp.max(scores, axis=0, keepdims=True))
                shrink = jnp.exp2(top_ref[...] - top)
                weights = jnp.exp2(scores - top)
                top_ref[...] = top
                sum_ref[...] = sum_ref[...] * shrink + jnp.sum(weights, axis=0, keepdims=True)
                acc_ref[...] = acc_ref[...] * shrink + dot(
                    kvs_ref[b, ROWS + group * HD : ROWS + group * HD + HD, :], weights.astype(BF)
                )

            context_ref[pl.ds(pl.multiple_of(head * HD, HD), HD), :] = acc_ref[...] / sum_ref[...]


STEP = 2048
STEPS = FF // STEP
LATE = (3, 3)


def last_kernel(
    moves,
    rate_s,
    tok_ref,
    gain_ref,
    q_ref,
    part_ref,
    pay_ref,
    w_out_hbm,
    w_obs_hbm,
    w_up_hbm,
    w_down_hbm,
    *rest,
):
    blocks = rest[:LON]
    count = sum(LATE)
    late = rest[LON : LON + count]
    (
        out_ref,
        w_out_ref,
        w_obs_ref,
        w_up_ref,
        w_down_ref,
        key_ref,
        value_ref,
        context_ref,
        largest_ref,
        ahead_ref,
        top_ref,
        sum_ref,
        acc_ref,
        kvs_ref,
        sem,
        spare,
    ) = rest[LON + count :]
    copies = [
        pltpu.make_async_copy(w_out_hbm, w_out_ref, sem.at[0]),
        pltpu.make_async_copy(w_obs_hbm, w_obs_ref, sem.at[1]),
    ]
    for s in range(STEPS):
        here = pl.ds(s * STEP, STEP)
        copies.append(pltpu.make_async_copy(w_up_hbm.at[:, here], w_up_ref.at[s], sem.at[2 + 2 * s]))
        copies.append(
            pltpu.make_async_copy(w_down_hbm.at[here, :], w_down_ref.at[s], sem.at[3 + 2 * s])
        )
    for copy in copies:
        copy.start()

    aheads = ahead_of(moves)
    lay_out(late, aheads[LON - count :], None, key_ref, value_ref)
    largest_ref[...] = jnp.zeros((1, ROWS), F32)

    @pl.loop(0, KVH)
    def _(group):
        for i in range(4):
            head = group * 4 + i
            total = attend(
                part_ref[head], group, head, LATE, None, rate_s, q_ref, key_ref, value_ref
            )
            weight_sum = total[HD : HD + 1]
            largest_ref[...] = jnp.maximum(largest_ref[...], weight_sum)
            context_ref[pl.ds(pl.multiple_of(head * HD, HD), HD), :] = total[:HD] * (
                1.0 / weight_sum
            )

    @pl.when(jnp.logical_not(jnp.max(largest_ref[...]) < 2.0**100))
    def _():
        careful(
            blocks,
            aheads,
            rate_s,
            q_ref,
            kvs_ref,
            ahead_ref,
            context_ref,
            top_ref,
            sum_ref,
            acc_ref,
            spare,
        )

    pay = jnp.concatenate([pay_ref[:, 0, :], pay_ref[:, 1, :]], axis=0)
    cell = pay[:, D:PAY].astype(F32).T
    cell = jnp.broadcast_to(cell[0:1, :], (ROWS, SLOTS)).astype(I32)
    place = (iota((ROWS, SLOTS), 0) + 1 == cell).astype(F32).astype(BF)
    pooled = dot(place, pay[:, 0:D]).astype(BF)
    context = context_ref[...].T.astype(BF)
    copies[0].wait()
    mixed = tok_ref[...].astype(F32) + dot(context, w_out_ref[...])
    copies[1].wait()
    mixed = (mixed + dot(pooled, w_obs_ref[...])).astype(BF).astype(F32)
    normed = normed_rows(mixed, gain_ref[...])
    for copy in copies[2:]:
        copy.wait()
    for s in range(STEPS):
        hidden = (0.5 * twice_gelu(dot(normed, w_up_ref[s]))).astype(BF)
        mixed = mixed + dot(hidden, w_down_ref[s])
    out_ref[...] = mixed.astype(BF)


def last_call(moves, head_rate, tokens, gain, q, part, pay, w_out, w_obs_out, w_up, w_down, blocks):
    return pl.pallas_call(
        functools.partial(last_kernel, moves),
        out_shape=jax.ShapeDtypeStruct((ROWS, D), BF),
        in_specs=[SMEM] + [VMEM] * 5 + [ANY] * (4 + LON) + [VMEM] * sum(LATE),
        out_specs=VMEM,
        scratch_shapes=[
            pltpu.VMEM((D, D), BF),
            pltpu.VMEM((D, D), BF),
            pltpu.VMEM((STEPS, D, STEP), BF),
            pltpu.VMEM((STEPS, STEP, D), BF),
            pltpu.VMEM((KVH, sum(LATE) * ROWS, 128), BF),
            pltpu.VMEM((KVH, VT, sum(LATE) * ROWS), BF),
            pltpu.VMEM((D, ROWS), F32),
            pltpu.VMEM((1, ROWS), F32),
            pltpu.SMEM((LON,), I32),
            pltpu.VMEM((1, ROWS), F32),
            pltpu.VMEM((1, ROWS), F32),
            pltpu.VMEM((HD, ROWS), F32),
            pltpu.VMEM((LON, 2 * ROWS, KVH * HD), BF),
            pltpu.SemaphoreType.DMA((2 + 2 * STEPS,)),
            pltpu.SemaphoreType.DMA,
        ],
        compiler_params=params(60),
        cost_estimate=cost(17),
        name="late_rows_project_update_mlp",
    )(
        head_rate,
        tokens,
        gain.reshape(1, D),
        q,
        part,
        pay,
        w_out,
        w_obs_out,
        w_up,
        w_down,
        *blocks,
        *blocks[LON - sum(LATE) :],
    )


def lon_of(x, z, core):
    return x * 8 + (z % 4) * 2 + core


def send(block, flip_x, step_z, flip_core):
    pairs = [
        (lon_of(x, z, core), lon_of(x ^ flip_x, z + step_z, core ^ flip_core))
        for x in range(2)
        for z in range(4)
        for core in range(2)
    ]
    return lax.ppermute(block, "lon", pairs)


def ahead_of(moves):
    me = lax.axis_index("lon")
    x, z, core = me // 8, (me // 2) % 4, me % 2
    sources = [
        lax.rem(x + fx, 2) * 8 + lax.rem(z + 4 - dz, 4) * 2 + lax.rem(core + fc, 2)
        for fx, dz, fc in moves
    ]
    return [lax.rem(s - me + LON, LON) for s in sources]


def shards(
    tokens,
    attn_gain,
    w_query,
    w_key,
    w_value,
    w_out,
    head_rate,
    obs_values,
    tile_owner,
    tile_cell,
    tile_count,
    w_obs_in,
    w_obs_out,
    mlp_gain,
    w_up,
    w_down,
):
    normed, kv = kv_call(tokens, attn_gain, w_key, w_value)
    up = send(kv, 0, 1, 0)
    down = send(kv, 0, 3, 0)
    across = send(kv, 1, 0, 0)
    far = send(kv, 0, 2, 0)
    sibling = send(kv, 0, 0, 1)
    pay = pool_call(obs_values, tile_owner, tile_cell, tile_count, w_obs_in)
    pay, normed, up, down, across, far, sibling = lax.optimization_barrier(
        (pay, normed, up, down, across, far, sibling)
    )
    late = [send(across, 0, 1, 0), send(across, 0, 3, 0), send(far, 1, 0, 0)]
    near = [across, up, down, far]
    near_twin = [send(b, 0, 0, 1) for b in near]
    pay = lax.all_to_all(pay, ("lat", "lon"), split_axis=0, concat_axis=0, tiled=True)
    late_twin = [send(b, 0, 0, 1) for b in late]

    near_moves = [(1, 0, 0), (0, 1, 0), (0, 3, 0), (0, 2, 0)]
    late_moves = [(1, 1, 0), (1, 3, 0), (1, 2, 0)]
    near_moves = near_moves + [(0, 0, 1)] + [(x, z, 1) for x, z, _ in near_moves]
    late_moves = late_moves + [(x, z, 1) for x, z, _ in late_moves]
    near = near + [sibling] + near_twin
    q, part = first_call(near_moves, head_rate, normed, w_query, kv, near)
    return last_call(
        [(0, 0, 0)] + near_moves + late_moves,
        head_rate,
        tokens,
        mlp_gain,
        q,
        part,
        pay,
        w_out,
        w_obs_out,
        w_up,
        w_down,
        [kv] + near + late + late_twin,
    )


def solution(mesh):
    shard = P(("lat", "lon"))
    rows = P(("lat", "lon"), None)
    return jax.shard_map(
        shards,
        mesh=mesh,
        in_specs=(rows,)
        + (P(),) * 6
        + (P(("lat", "lon"), None, None), rows, shard, shard)
        + (P(),) * 5,
        out_specs=rows,
        check_vma=False,
    )
```

```python
import functools
import math

import jax
import jax.numpy as jnp
from jax import lax
from jax.experimental import pallas as pl
from jax.experimental.pallas import tpu as pltpu
from jax.sharding import PartitionSpec as P

BF = jnp.bfloat16
F32 = jnp.float32
I32 = jnp.int32

D = 1024
HEADS = 16
HD = 64
KVH = 4
FF = 4096
ROWS = 256
TILES = 128
TROWS = 128
F_OBS = 32
LON = 16
BAND = ROWS * LON
SLOTS = 256
PAY = D + 128
LOG2E = 1.4426950408889634
VT = HD + 16
MIB = 2**20
VMEM = pl.BlockSpec(memory_space=pltpu.VMEM)
SMEM = pl.BlockSpec(memory_space=pltpu.SMEM)
ANY = pl.BlockSpec(memory_space=pl.ANY)


def iota(shape, dim):
    return lax.broadcasted_iota(I32, shape, dim)


def params(mib):
    return pltpu.CompilerParams(vmem_limit_bytes=mib * MIB)


def cost(micros):
    return pl.CostEstimate(
        flops=int(micros * 1.0e9), bytes_accessed=int(micros * 1.0e6), transcendentals=0
    )


def dot(a, b):
    return jnp.dot(a, b, preferred_element_type=F32)


def normed_rows(rows, gain):
    mean_square = jnp.mean(rows * rows, axis=-1, keepdims=True)
    return (rows * lax.rsqrt(mean_square + 1e-05) * gain).astype(BF)


def twice_gelu(x):
    k0 = math.sqrt(2.0 / math.pi)
    k1 = k0 * 0.044715
    inner = x * (x * x * k1 + k0)
    return jnp.tanh(inner) * x + x


def kv_kernel(tok_ref, gain_ref, wk_ref, wv_ref, normed_ref, kv_ref):
    normed = normed_rows(tok_ref[...].astype(F32), gain_ref[...])
    normed_ref[...] = normed
    kv_ref[0:ROWS, :] = dot(normed, wk_ref[...]).astype(BF)
    kv_ref[ROWS : 2 * ROWS, :] = dot(normed, wv_ref[...]).T.astype(BF)


def kv_call(tokens, gain, w_key, w_value):
    return pl.pallas_call(
        kv_kernel,
        out_shape=(
            jax.ShapeDtypeStruct((ROWS, D), BF),
            jax.ShapeDtypeStruct((2 * ROWS, KVH * HD), BF),
        ),
        in_specs=[VMEM] * 4,
        out_specs=(VMEM, VMEM),
        compiler_params=params(60),
        cost_estimate=cost(3),
        name="norm_keys_values",
    )(tokens, gain.reshape(1, D), w_key, w_value)


BLOCK = 512
HALF = BLOCK // 2
COLS = 512


def pool_kernel(
    cnt_s, obs_ref, cnt_ref, own_ref, cell_ref, w_ref, pay_ref, live_ref, acc_ref, act_ref, member_ref
):
    square = (TILES, TILES)
    lanes = [(iota(square, 1) // F_OBS == k).astype(F32).astype(BF) for k in range(4)]
    column = iota(square, 1)

    def put(step, first):
        for u in range(4):
            four = step * 4 + u
            counts = [cnt_s[four * 4 + k] for k in range(4)]
            limit = jnp.concatenate([jnp.full((F_OBS, TROWS), c, I32) for c in counts], axis=0)
            rows = obs_ref[pl.ds(pl.multiple_of(four * TILES, TILES), TILES), :]
            rows = jnp.where(column < limit, rows, jnp.zeros_like(rows)).T
            for k, count in enumerate(counts):
                live_ref[pl.ds(pl.multiple_of(first, 32), TROWS), :] = rows * lanes[k]
                first = first + ((count + 31) // 32) * 32
        return first

    total = lax.fori_loop(0, TILES // 16, put, jnp.int32(0))
    for i in range(0, 2 * BLOCK, 128):
        live_ref[pl.ds(pl.multiple_of(total + i, 32), 128), :] = jnp.zeros(square, BF)

    weights = jnp.concatenate([w_ref[...]] * 4, axis=0)
    cnt = jnp.broadcast_to(cnt_ref[...].astype(F32), square).T
    groups = jnp.floor((cnt + 31.0) * (1.0 / 32.0))
    earlier = (iota(square, 1) < iota(square, 0)).astype(F32)
    start = dot(earlier.astype(BF), groups.astype(BF)) * 16.0
    start = jnp.concatenate([start] * (HALF // 128), axis=1)
    length = jnp.concatenate([groups * 16.0] * (HALF // 128), axis=1)

    acc_ref[...] = jnp.zeros_like(acc_ref)
    act_ref[...] = jnp.zeros_like(act_ref)
    member_ref[...] = jnp.zeros_like(member_ref)

    def one_block(block, now):
        old = 1 - now
        rows = live_ref[pl.ds(pl.multiple_of(block * BLOCK, BLOCK), BLOCK), :]
        place = (iota((TILES, HALF), 1) + block * HALF).astype(F32) - start
        member_ref[now] = ((place >= 0) & (place < length)).astype(F32).astype(BF)
        for c in range(0, D, COLS):
            here = slice(c, c + COLS)
            x = dot(rows, weights[:, here])
            acc_ref[:, here] += dot(member_ref[old], act_ref[old, :, here])
            act = twice_gelu(x.astype(BF))
            act_ref[now, :, here] = jnp.concatenate(
                [act[i : i + 16] + act[i + 16 : i + 32] for i in range(0, BLOCK, 32)], axis=0
            )

    @pl.loop(0, (total + 2 * BLOCK - 1) // (2 * BLOCK))
    def _(pair):
        one_block(2 * pair, 0)
        one_block(2 * pair + 1, 1)

    pooled = (acc_ref[...] + dot(member_ref[1], act_ref[1])) * (0.5 / cnt[:, 0:1])
    own_t = jnp.broadcast_to(own_ref[...].astype(F32), square)
    rank = jnp.sum(
        jnp.where((own_t.T == own_t) & (iota(square, 0) < iota(square, 1)), 1.0, 0.0),
        axis=0,
        keepdims=True,
    )
    slot = (2.0 * own_t[0:1, :] + rank).astype(I32)
    cell = (jnp.broadcast_to(cell_ref[...].astype(F32), square).T + 1.0).astype(BF)
    for k in range(2):
        place = (2 * iota(square, 0) + k == slot).astype(F32).astype(BF)
        pay_ref[:, k, 0:D] = dot(place, pooled.astype(BF)).astype(BF)
        pay_ref[:, k, D:PAY] = dot(place, cell).astype(BF)


def pool_call(obs_values, tile_owner, tile_cell, tile_count, w_obs_in):
    return pl.pallas_call(
        pool_kernel,
        out_shape=jax.ShapeDtypeStruct((SLOTS // 2, 2, PAY), BF),
        in_specs=[SMEM] + [VMEM] * 5,
        out_specs=VMEM,
        scratch_shapes=[
            pltpu.VMEM((TILES * TROWS + 2 * BLOCK, 128), BF),
            pltpu.VMEM((TILES, D), F32),
            pltpu.VMEM((2, HALF, D), BF),
            pltpu.VMEM((2, TILES, HALF), BF),
        ],
        compiler_params=params(60),
        cost_estimate=cost(15),
        name="pool_tiles",
    )(
        tile_count,
        jnp.transpose(obs_values, (0, 2, 1)).reshape(TILES * F_OBS, TROWS),
        tile_count.reshape(1, TILES),
        tile_owner.reshape(1, TILES),
        tile_cell.reshape(1, TILES),
        w_obs_in,
    )


def three(x):
    hi = x.astype(BF)
    rest = x - hi.astype(F32)
    mid = rest.astype(BF)
    lo = (rest - mid.astype(F32)).astype(BF)
    return [hi.astype(F32), mid.astype(F32), lo.astype(F32)]


def stacked(rows, count):
    place = iota((count, ROWS), 0)
    out = jnp.zeros((count, ROWS), F32)
    for i, row in enumerate(rows):
        out = jnp.where(place == i, jnp.broadcast_to(row, out.shape), out)
    return out


def value_rows(kv_ref, group):
    first = ROWS + group * HD
    return jnp.concatenate([kv_ref[first : first + HD, :], jnp.ones((VT - HD, ROWS), BF)], axis=0)


def place_lanes(first):
    lane = iota((ROWS, 128), 1) - first
    row = iota((ROWS, 128), 0)

    def lanes(low, value):
        return jnp.where((lane >= low) & (lane < low + 3), value, 0)

    parts = (lanes(0, -row) + lanes(6, 1), lanes(0, row) + lanes(9, 1), lanes(12, 1), lanes(3, -ROWS))
    return [p.astype(F32).astype(BF) for p in parts]


def beside_keys(parts, ahead):
    blocks = jnp.where(ahead < 8, ahead, LON - ahead).astype(F32)
    blocks = jnp.full((ROWS, 128), blocks, F32).astype(BF)
    return jnp.where(ahead < 8, parts[0], parts[1]) + parts[3] * blocks


def lay_out(blocks, aheads, half_way, key_ref, value_ref):
    lane = iota((ROWS, 128), 1)
    parts = (place_lanes(HD), place_lanes(0))
    for b, block in enumerate(blocks):
        here = pl.ds(b * ROWS, ROWS)
        extra = [p[2] if b == half_way else beside_keys(p, aheads[b]) for p in parts]
        for group in range(KVH):
            odd = group % 2
            pair = block[0:ROWS, (group // 2) * 128 : (group // 2) * 128 + 128]
            key_ref[group, here, :] = jnp.where((lane < HD) == (odd == 0), pair, extra[odd])
            value_ref[group, :, here] = value_rows(block, group)


def attend(total, group, head, chunks, gap, rate_s, q_ref, key_ref, value_ref):
    first = 0
    for size in chunks:
        here = pl.ds(first * ROWS, size * ROWS)
        scores = dot(key_ref[group, here, :], q_ref[head])
        if gap is not None and first == 0:
            far = scores[:ROWS] - (rate_s[head] * LOG2E) * gap
            scores = jnp.concatenate([far, scores[ROWS:]], axis=0)
        total = total + dot(value_ref[group, :, here], jnp.exp2(scores).astype(BF))
        first = first + size
    return total


NEAR = (5, 4)


def first_kernel(moves, rate_s, normed_ref, wq_ref, kv_ref, *rest):
    blocks = rest[: len(moves)]
    q_ref, out_ref, dist_ref, key_ref, value_ref = rest[len(moves) :]
    q = (dot(normed_ref[...], wq_ref[...]) * (0.125 * LOG2E)).T
    dist_ref[...] = jnp.abs(iota((ROWS, ROWS), 0) - iota((ROWS, ROWS), 1)).astype(F32)
    lane = iota((ROWS, 128), 1)
    at = iota((1, ROWS), 1).astype(F32)
    for group in range(KVH):
        even = group % 2 == 0
        pair = kv_ref[0:ROWS, (group // 2) * 128 : (group // 2) * 128 + 128]
        keys = jnp.where((lane < HD) == even, pair, jnp.zeros_like(pair))
        values = value_rows(kv_ref, group)
        for head in range(4 * group, 4 * group + 4):
            rate = rate_s[head] * LOG2E
            own = q[head * HD : head * HD + HD, :].astype(BF)
            blank = jnp.zeros((HD, ROWS), BF)
            scores = dot(keys, jnp.concatenate([own, blank] if even else [blank, own], axis=0))
            scores = scores - rate * dist_ref[...]
            top = jnp.max(scores, axis=0, keepdims=True)
            out_ref[head] = dot(values, jnp.exp2(scores - top).astype(BF))
            rates = three(jnp.full((1, ROWS), rate, F32))
            extra = stacked(
                rates + rates + three(rate * at - top) + three(-rate * at - top) + three(-top), 16
            ).astype(BF)
            extra = jnp.concatenate([extra, jnp.zeros((HD - 16, ROWS), BF)], axis=0)
            q_ref[head] = jnp.concatenate([own, extra] if even else [extra, own], axis=0)

    lay_out(blocks, ahead_of(moves), 0, key_ref, value_ref)
    gap = LON // 2 * ROWS - dist_ref[...]

    @pl.loop(0, KVH)
    def _(group):
        for i in range(4):
            head = group * 4 + i
            out_ref[head] = attend(
                out_ref[head], group, head, NEAR, gap, rate_s, q_ref, key_ref, value_ref
            )


def first_call(moves, head_rate, normed, w_query, kv, blocks):
    count = len(blocks)
    return pl.pallas_call(
        functools.partial(first_kernel, moves),
        out_shape=(
            jax.ShapeDtypeStruct((HEADS, 128, ROWS), BF),
            jax.ShapeDtypeStruct((HEADS, VT, ROWS), F32),
        ),
        in_specs=[SMEM] + [VMEM] * (3 + count),
        out_specs=(VMEM, VMEM),
        scratch_shapes=[
            pltpu.VMEM((ROWS, ROWS), F32),
            pltpu.VMEM((KVH, count * ROWS, 128), BF),
            pltpu.VMEM((KVH, VT, count * ROWS), BF),
        ],
        compiler_params=params(60),
        cost_estimate=cost(18),
        name="queries_near_rows",
    )(head_rate, normed, w_query, kv, *blocks)


def careful(
    blocks, aheads, rate_s, q_ref, kvs_ref, ahead_ref, context_ref, top_ref, sum_ref, acc_ref, sem
):
    for b in range(LON):
        ahead_ref[b] = aheads[b]
        copy = pltpu.make_async_copy(blocks[b], kvs_ref.at[b], sem)
        copy.start()
        copy.wait()
    lane = iota((ROWS, 128), 1)
    for group in range(KVH):

        @pl.loop(0, 4)
        def _(i):
            head = group * 4 + i
            top_ref[...] = jnp.full((1, ROWS), -jnp.inf, F32)
            sum_ref[...] = jnp.zeros((1, ROWS), F32)
            acc_ref[...] = jnp.zeros((HD, ROWS), F32)

            @pl.loop(0, LON)
            def _(b):
                keys = kvs_ref[b, 0:ROWS, (group // 2) * 128 : (group // 2) * 128 + 128]
                keys = jnp.where((lane < HD) == (group % 2 == 0), keys, jnp.zeros_like(keys))
                gap = jnp.abs(ahead_ref[b] * ROWS + iota((ROWS, ROWS), 0) - iota((ROWS, ROWS), 1))
                gap = jnp.minimum(gap, BAND - gap).astype(F32)
                scores = dot(keys, q_ref[head]) - (rate_s[head] * LOG2E) * gap
                top = jnp.maximum(top_ref[...], jnp.max(scores, axis=0, keepdims=True))
                shrink = jnp.exp2(top_ref[...] - top)
                weights = jnp.exp2(scores - top)
                top_ref[...] = top
                sum_ref[...] = sum_ref[...] * shrink + jnp.sum(weights, axis=0, keepdims=True)
                acc_ref[...] = acc_ref[...] * shrink + dot(
                    kvs_ref[b, ROWS + group * HD : ROWS + group * HD + HD, :], weights.astype(BF)
                )

            context_ref[pl.ds(pl.multiple_of(head * HD, HD), HD), :] = acc_ref[...] / sum_ref[...]


STEP = 2048
STEPS = FF // STEP
LATE = (4, 2)


def last_kernel(
    moves,
    rate_s,
    tok_ref,
    gain_ref,
    q_ref,
    part_ref,
    pay_ref,
    w_out_hbm,
    w_obs_hbm,
    w_up_hbm,
    w_down_hbm,
    *rest,
):
    blocks = rest[:LON]
    count = sum(LATE)
    late = rest[LON : LON + count]
    (
        out_ref,
        w_out_ref,
        w_obs_ref,
        w_up_ref,
        w_down_ref,
        key_ref,
        value_ref,
        context_ref,
        largest_ref,
        ahead_ref,
        top_ref,
        sum_ref,
        acc_ref,
        kvs_ref,
        sem,
        spare,
    ) = rest[LON + count :]
    copies = [
        pltpu.make_async_copy(w_out_hbm, w_out_ref, sem.at[0]),
        pltpu.make_async_copy(w_obs_hbm, w_obs_ref, sem.at[1]),
    ]
    for s in range(STEPS):
        here = pl.ds(s * STEP, STEP)
        copies.append(pltpu.make_async_copy(w_up_hbm.at[:, here], w_up_ref.at[s], sem.at[2 + 2 * s]))
        copies.append(
            pltpu.make_async_copy(w_down_hbm.at[here, :], w_down_ref.at[s], sem.at[3 + 2 * s])
        )
    for copy in copies:
        copy.start()

    aheads = ahead_of(moves)
    lay_out(late, aheads[LON - count :], None, key_ref, value_ref)
    largest_ref[...] = jnp.zeros((1, ROWS), F32)

    @pl.loop(0, KVH)
    def _(group):
        for i in range(4):
            head = group * 4 + i
            total = attend(
                part_ref[head], group, head, LATE, None, rate_s, q_ref, key_ref, value_ref
            )
            weight_sum = total[HD : HD + 1]
            largest_ref[...] = jnp.maximum(largest_ref[...], weight_sum)
            context_ref[pl.ds(pl.multiple_of(head * HD, HD), HD), :] = total[:HD] * (
                1.0 / weight_sum
            )

    @pl.when(jnp.logical_not(jnp.max(largest_ref[...]) < 2.0**100))
    def _():
        careful(
            blocks,
            aheads,
            rate_s,
            q_ref,
            kvs_ref,
            ahead_ref,
            context_ref,
            top_ref,
            sum_ref,
            acc_ref,
            spare,
        )

    pay = jnp.concatenate([pay_ref[:, 0, :], pay_ref[:, 1, :]], axis=0)
    cell = pay[:, D:PAY].astype(F32).T
    cell = jnp.broadcast_to(cell[0:1, :], (ROWS, SLOTS)).astype(I32)
    place = (iota((ROWS, SLOTS), 0) + 1 == cell).astype(F32).astype(BF)
    pooled = dot(place, pay[:, 0:D]).astype(BF)
    context = context_ref[...].T.astype(BF)
    copies[0].wait()
    mixed = tok_ref[...].astype(F32) + dot(context, w_out_ref[...])
    copies[1].wait()
    mixed = (mixed + dot(pooled, w_obs_ref[...])).astype(BF).astype(F32)
    normed = normed_rows(mixed, gain_ref[...])
    for copy in copies[2:]:
        copy.wait()
    for s in range(STEPS):
        hidden = (0.5 * twice_gelu(dot(normed, w_up_ref[s]))).astype(BF)
        mixed = mixed + dot(hidden, w_down_ref[s])
    out_ref[...] = mixed.astype(BF)


def last_call(moves, head_rate, tokens, gain, q, part, pay, w_out, w_obs_out, w_up, w_down, blocks):
    return pl.pallas_call(
        functools.partial(last_kernel, moves),
        out_shape=jax.ShapeDtypeStruct((ROWS, D), BF),
        in_specs=[SMEM] + [VMEM] * 5 + [ANY] * (4 + LON) + [VMEM] * sum(LATE),
        out_specs=VMEM,
        scratch_shapes=[
            pltpu.VMEM((D, D), BF),
            pltpu.VMEM((D, D), BF),
            pltpu.VMEM((STEPS, D, STEP), BF),
            pltpu.VMEM((STEPS, STEP, D), BF),
            pltpu.VMEM((KVH, sum(LATE) * ROWS, 128), BF),
            pltpu.VMEM((KVH, VT, sum(LATE) * ROWS), BF),
            pltpu.VMEM((D, ROWS), F32),
            pltpu.VMEM((1, ROWS), F32),
            pltpu.SMEM((LON,), I32),
            pltpu.VMEM((1, ROWS), F32),
            pltpu.VMEM((1, ROWS), F32),
            pltpu.VMEM((HD, ROWS), F32),
            pltpu.VMEM((LON, 2 * ROWS, KVH * HD), BF),
            pltpu.SemaphoreType.DMA((2 + 2 * STEPS,)),
            pltpu.SemaphoreType.DMA,
        ],
        compiler_params=params(60),
        cost_estimate=cost(17),
        name="late_rows_project_update_mlp",
    )(
        head_rate,
        tokens,
        gain.reshape(1, D),
        q,
        part,
        pay,
        w_out,
        w_obs_out,
        w_up,
        w_down,
        *blocks,
        *blocks[LON - sum(LATE) :],
    )


def lon_of(x, z, core):
    return x * 8 + (z % 4) * 2 + core


def send(block, flip_x, step_z, flip_core):
    pairs = [
        (lon_of(x, z, core), lon_of(x ^ flip_x, z + step_z, core ^ flip_core))
        for x in range(2)
        for z in range(4)
        for core in range(2)
    ]
    return lax.ppermute(block, "lon", pairs)


def ahead_of(moves):
    me = lax.axis_index("lon")
    x, z, core = me // 8, (me // 2) % 4, me % 2
    sources = [
        lax.rem(x + fx, 2) * 8 + lax.rem(z + 4 - dz, 4) * 2 + lax.rem(core + fc, 2)
        for fx, dz, fc in moves
    ]
    return [lax.rem(s - me + LON, LON) for s in sources]


def shards(
    tokens,
    attn_gain,
    w_query,
    w_key,
    w_value,
    w_out,
    head_rate,
    obs_values,
    tile_owner,
    tile_cell,
    tile_count,
    w_obs_in,
    w_obs_out,
    mlp_gain,
    w_up,
    w_down,
):
    normed, kv = kv_call(tokens, attn_gain, w_key, w_value)
    up = send(kv, 0, 1, 0)
    down = send(kv, 0, 3, 0)
    across = send(kv, 1, 0, 0)
    far = send(kv, 0, 2, 0)
    sibling = send(kv, 0, 0, 1)
    pay = pool_call(obs_values, tile_owner, tile_cell, tile_count, w_obs_in)
    pay, normed, up, down, across, far, sibling = lax.optimization_barrier(
        (pay, normed, up, down, across, far, sibling)
    )
    late = [send(across, 0, 1, 0), send(across, 0, 3, 0), send(far, 1, 0, 0)]
    near = [across, up, down, far]
    near_twin = [send(b, 0, 0, 1) for b in near]
    pay = lax.all_to_all(pay, ("lat", "lon"), split_axis=0, concat_axis=0, tiled=True)
    late_twin = [send(b, 0, 0, 1) for b in late]

    near_moves = [(1, 0, 0), (0, 1, 0), (0, 3, 0), (0, 2, 0)]
    late_moves = [(1, 1, 0), (1, 3, 0), (1, 2, 0)]
    near_moves = near_moves + [(0, 0, 1)] + [(x, z, 1) for x, z, _ in near_moves]
    late_moves = late_moves + [(x, z, 1) for x, z, _ in late_moves]
    near = near + [sibling] + near_twin
    q, part = first_call(near_moves, head_rate, normed, w_query, kv, near)
    return last_call(
        [(0, 0, 0)] + near_moves + late_moves,
        head_rate,
        tokens,
        mlp_gain,
        q,
        part,
        pay,
        w_out,
        w_obs_out,
        w_up,
        w_down,
        [kv] + near + late + late_twin,
    )


def solution(mesh):
    shard = P(("lat", "lon"))
    rows = P(("lat", "lon"), None)
    return jax.shard_map(
        shards,
        mesh=mesh,
        in_specs=(rows,)
        + (P(),) * 6
        + (P(("lat", "lon"), None, None), rows, shard, shard)
        + (P(),) * 5,
        out_specs=rows,
        check_vma=False,
    )
```
